128 devices in a mesh: row: 8 (over y, x_hi), col: 16 (over x_lo, z, core).
Axes of the slice: x: 4 (x_hi: 2, x_lo: 2; x = x_hi * 2 + x_lo), y: 4, z: 4, core: 2. Of those that a mesh axis runs over, the one named last changes fastest.
Arguments:
- features: float32 [32768, 256], P(('row', 'col')), may hold values from -6 to 6
- weight: float32 [256, 256], replicated, may hold values from -0.375 to 0.375
- tile_vals: float32 [16, 8, 256, 128, 128], P('col', 'row'), may hold values from 0 to 0.022097087
- tile_index: int32 [16, 8, 2, 256], P('col', 'row'), may hold values from 0 to 31, as said below
- tile_count: int32 [16, 8], P('col', 'row'), may hold values from 1 to 256, as said below
- out_grad: float32 [32768, 256], P(('col', 'row')), may hold values from -6 to 6
Outputs:
- hidden: float32 [32768, 256], P(('col', 'row'))
- grad_x: float32 [32768, 256], P(('row', 'col'))
- grad_w: float32 [256, 256], replicated
The draws below stay inside these ranges and needn't reach their ends.
Inputs may be any that keep to these rules, and one draw needn't show every extreme that they name: For each device the first tile_count slots name distinct tiles; tile_index[c, r, 0, s] is below 16 and tile_index[c, r, 1, s] below 32. `tile_count`: exactly one device holds 256 tiles in every draw.
All inputs are finite; a program needn't handle non-finite values.
Results may differ from the reference program's by a relative error of at most 0.0003.
Values sent between devices are 32-bit elements; how exact they have to be, the bound alone decides.
No kernel may reach another device: no remote copies, remote signals or barrier semaphores. Data moves between devices by JAX's collectives and lax.ppermute only.
A program may use at most 128 MiB of HBM per device.

```python
import jax
import jax.numpy as jnp
from jax import lax

FEAT = 256
TILE = 128
TR = 16
MAXT = 256
TC = 32
NODES = 32768
N_ROW = 8
N_COL = 16


def draw_tile_index(key, part):
    key = jax.random.fold_in(key, 17)
    places = TR * TC
    scores = jax.random.randint(key, (N_COL, N_ROW, places), 0, 16384)
    ranked = scores * places + jnp.arange(places, dtype=jnp.int32)
    top_scores, chosen = lax.top_k(ranked, MAXT)
    chosen = chosen.astype(jnp.int32)
    return jnp.stack([chosen // TC, chosen % TC], axis=2).astype(jnp.int32)


def draw_tile_count(key, part):
    key = jax.random.fold_in(key, 29)
    hub_keys = jax.random.split(key, 3)
    hub_col = jax.random.randint(hub_keys[0], (), 0, N_COL)
    hub_row = jax.random.randint(hub_keys[1], (), 0, N_ROW)
    extra = jax.random.randint(hub_keys[2], (N_COL, N_ROW), 0, 4)
    col_pos = jnp.arange(N_COL, dtype=jnp.int32)[:, None]
    row_pos = jnp.arange(N_ROW, dtype=jnp.int32)[None, :]
    distance = jnp.abs(col_pos - hub_col) + jnp.abs(row_pos - hub_row)
    extra = jnp.where(distance == 0, 0, extra)
    return jnp.maximum(MAXT * 4 // (4 + distance + extra), 1).astype(jnp.int32)


def block_levels(stream_key, extent, pieces, low, top_value):
    def one(position, shards_of):
        steps = jax.random.uniform(jax.random.fold_in(jax.random.fold_in(stream_key, 6), position), (shards_of,), jnp.float32, low / len(pieces), top_value / len(pieces))
        return jnp.repeat(jnp.exp(steps), extent[position] // shards_of).reshape((-1,) + (1,) * (len(extent) - position - 1))

    loudness = one(*pieces[0])
    for cut in pieces[1:]:
        loudness = loudness * one(*cut)
    return loudness


def centred(stream_key, shape, scale, reach, shards=(), held_as=jnp.bfloat16):
    result = jax.random.normal(stream_key, shape, jnp.float32) * scale
    if len(shards) > 0:
        result = block_levels(stream_key, shape, shards, -0.22, 0.18) * result
    return jnp.clip(result, min=-reach, max=reach).astype(held_as)


def setup_inputs(seed: int = 0) -> dict:
    splits = jax.random.split(jax.random.key(seed), 7)
    features = centred(splits[0], (NODES, FEAT), 1.0, 6.0, ((0, 128),), jnp.float32)
    weight = centred(splits[1], (FEAT, FEAT), FEAT ** -0.5, 0.375, (), jnp.float32)
    tile_vals = jnp.clip(0.022097087 * jax.random.uniform(splits[2], (N_COL, N_ROW, MAXT, TILE, TILE), jnp.float32) ** block_levels(splits[2], (N_COL, N_ROW, MAXT, TILE, TILE), ((0, 16), (1, 8)), -0.2, 0.2), 0.0, 0.022097087)
    tile_index = draw_tile_index(jax.random.fold_in(splits[6], 71), 0)
    tile_count = draw_tile_count(jax.random.fold_in(splits[6], 71), 0)
    out_grad = centred(splits[5], (NODES, FEAT), 1.0, 6.0, ((0, 128),), jnp.float32)
    return dict(features=features, weight=weight, tile_vals=tile_vals, tile_index=tile_index, tile_count=tile_count, out_grad=out_grad)


highest = lax.Precision.HIGHEST


def silu_slope(value):
    sigma = jax.nn.sigmoid(value)
    return sigma * (1.0 + value * (1.0 - sigma))


def spread(tile_vals, tile_index, tile_count, source, flipped):
    slot_ids = jnp.arange(MAXT, dtype=jnp.int32)
    device_ids = jnp.arange(N_COL * N_ROW, dtype=jnp.int32)
    col_pos = (device_ids // N_ROW).astype(jnp.int32)
    row_pos = (device_ids % N_ROW).astype(jnp.int32)
    stacked = (tile_vals.reshape(N_COL * N_ROW, MAXT, TILE, TILE),
               tile_index.reshape(N_COL * N_ROW, 2, MAXT),
               tile_count.reshape(N_COL * N_ROW), col_pos, row_pos)
    src_blocks = source.reshape(NODES // TILE, TILE, FEAT)
    einsum_form = "sji,sjf->sif" if flipped else "sij,sjf->sif"

    def device_step(summed, device_item):
        slot_tiles, slot_index, live_count, dest_block, src_block = device_item
        dest_ids = (dest_block * TR + slot_index[0]).astype(jnp.int32)
        src_ids = (src_block * TC + slot_index[1]).astype(jnp.int32)
        take_ids = dest_ids if flipped else src_ids
        put_ids = src_ids if flipped else dest_ids
        live_mask = (slot_ids < live_count).astype(jnp.float32)
        products = jnp.einsum(einsum_form, slot_tiles, src_blocks[take_ids], precision=highest)
        return summed.at[put_ids].add(products * live_mask[:, None, None]), None

    summed = jnp.zeros((NODES // TILE, TILE, FEAT), jnp.float32)
    summed, unused = lax.scan(device_step, summed, stacked)
    return summed.reshape(NODES, FEAT)


def reference(features, weight, tile_vals, tile_index, tile_count, out_grad):
    projected = jnp.dot(features, weight, precision=highest, preferred_element_type=jnp.float32)
    pre_act = spread(tile_vals, tile_index, tile_count, projected, False)
    hidden = pre_act * jax.nn.sigmoid(pre_act)
    grad_pre = out_grad * silu_slope(pre_act)
    grad_proj = spread(tile_vals, tile_index, tile_count, grad_pre, True)
    grad_x = jnp.dot(grad_proj, weight.T, precision=highest, preferred_element_type=jnp.float32)
    grad_w = jnp.dot(features.T, grad_proj, precision=highest, preferred_element_type=jnp.float32) * (NODES ** -0.5)
    return (hidden, grad_x, grad_w)
```

```python
import functools

import jax
import jax.numpy as jnp
from jax import lax
from jax.experimental import pallas as pl
from jax.experimental.pallas import tpu as pltpu
from jax.sharding import Mesh
from jax.sharding import PartitionSpec as P

EDGE = 128
GROUP = 64
UNROLL = 32
ROW_AXES = ("y", "xh")
COL_AXES = ("xl", "z", "core")
PLANE_AXES = ("xl", "z")
VMEM_LIMIT = 48 << 20


def split(value):
    high = value.astype(jnp.bfloat16)
    low = (value - high.astype(jnp.float32)).astype(jnp.bfloat16)
    return high, low


def dot3(left, right, dims=((1,), (0,))):
    dot = functools.partial(
        lax.dot_general, dimension_numbers=(dims, ((), ())), preferred_element_type=jnp.float32
    )
    left_high, left_low = split(left)
    right_high, right_low = split(right)
    return dot(left_high, right_high) + (dot(left_high, right_low) + dot(left_low, right_high))


def spread_body(flipped, n_src, take, put, count, tiles, *refs):
    sources, (outs, (paired, total)) = refs[:n_src], (refs[n_src:-2], refs[-2:])
    step = pl.program_id(0)

    @pl.when(step == 0)
    def _():
        total[...] = jnp.zeros_like(total)
        place = 0
        for source in sources:

            def pair(index, carry, source=source, place=place):
                high, low = split(source[index])
                paired[place + index, :EDGE, :EDGE] = high
                paired[place + index, :EDGE, EDGE:] = low
                paired[place + index, EDGE:, :EDGE] = high
                paired[place + index, EDGE:, EDGE:] = jnp.zeros_like(low)
                return carry

            lax.fori_loop(0, source.shape[0], pair, 0)
            place += source.shape[0]

    first = step * GROUP

    def one(slot):
        tile = tiles[slot]
        high, low = split(tile.T if flipped else tile)
        both = jnp.dot(
            jnp.concatenate([high, low], axis=1),
            paired[take[first + slot]],
            preferred_element_type=jnp.float32,
        )
        where = put[first + slot]
        total[where] += both[:, :EDGE] + both[:, EDGE:]

    live = jnp.clip(count[0] - first, 0, GROUP)
    blocks = live // UNROLL

    def block(index, carry):
        for offset in range(UNROLL):
            one(index * UNROLL + offset)
        return carry

    def rest(slot, carry):
        one(slot)
        return carry

    lax.fori_loop(0, blocks, block, 0)
    lax.fori_loop(blocks * UNROLL, live, rest, 0)

    @pl.when(step == pl.num_programs(0) - 1)
    def _():
        place = 0
        for out in outs:
            out[...] = total[place : place + out.shape[0]]
            place += out.shape[0]


def spread(tiles, take, put, count, sources, out_counts, flipped, name):
    slots = tiles.shape[0]
    src_count = sum(source.shape[0] for source in sources)
    whole = lambda *unused: (0, 0, 0)
    return pl.pallas_call(
        functools.partial(spread_body, flipped, len(sources)),
        grid_spec=pltpu.PrefetchScalarGridSpec(
            num_scalar_prefetch=3,
            grid=(slots // GROUP,),
            in_specs=[
                pl.BlockSpec(
                    (GROUP, EDGE, EDGE),
                    lambda g, take, put, count: (jnp.minimum(g, (count[0] - 1) // GROUP), 0, 0),
                )
            ]
            + [pl.BlockSpec(source.shape, whole) for source in sources],
            out_specs=[pl.BlockSpec((n, EDGE, EDGE), whole) for n in out_counts],
            scratch_shapes=[
                pltpu.VMEM((src_count, 2 * EDGE, 2 * EDGE), jnp.bfloat16),
                pltpu.VMEM((sum(out_counts), EDGE, EDGE), jnp.float32),
            ],
        ),
        out_shape=[jax.ShapeDtypeStruct((n, EDGE, EDGE), jnp.float32) for n in out_counts],
        compiler_params=pltpu.CompilerParams(vmem_limit_bytes=VMEM_LIMIT),
        cost_estimate=pl.CostEstimate(
            flops=2 * slots * EDGE * 4 * EDGE * EDGE,
            bytes_accessed=slots * EDGE * EDGE * 4,
            transcendentals=0,
        ),
        name=name,
    )(take, put, count, tiles, *sources)


def middle_body(terms0, terms1, weight, out_grad, hidden, grad0, grad1, gathered, grad_pre):
    parts = [jnp.sum(terms[...], axis=0) for terms in (terms0, terms1)]
    mixed = jnp.concatenate(parts, axis=1)
    gathered[...] = mixed
    pre_act = dot3(mixed, weight[...])
    sigma = jax.nn.sigmoid(pre_act)
    hidden[...] = pre_act * sigma
    slope = sigma * (1.0 + pre_act * (1.0 - sigma))
    local = out_grad[...] * slope
    grad_pre[...] = local
    back = dot3(local, weight[...], ((1,), (1,)))
    grad0[...] = back[:, :EDGE]
    grad1[...] = back[:, EDGE:]


def middle(terms0, terms1, weight, out_grad):
    rows, width = out_grad.shape
    full = jax.ShapeDtypeStruct((rows, width), jnp.float32)
    half = jax.ShapeDtypeStruct((rows, EDGE), jnp.float32)
    return pl.pallas_call(
        middle_body,
        out_shape=[full, half, half, full, full],
        compiler_params=pltpu.CompilerParams(vmem_limit_bytes=VMEM_LIMIT),
        name="middle",
    )(terms0, terms1, weight, out_grad)


def weight_body(gathered, grad_pre, out):
    out[...] = dot3(gathered[...], grad_pre[...], ((0,), (0,)))


def exchange(value, axes):
    return lax.all_to_all(value, axes, 0, 0, tiled=True)


def copies(value, count):
    return jnp.broadcast_to(value[None], (count, *value.shape))


def swap_core(value):
    return lax.ppermute(value, "core", [(0, 1), (1, 0)])


def body(features, weight, tile_vals, tile_index, tile_count, out_grad):
    tiles = tile_vals[0, 0]
    dest = tile_index[0, 0, 0]
    src = tile_index[0, 0, 1]
    count = tile_count[0]
    n_row = lax.axis_size(ROW_AXES)
    n_col = lax.axis_size(COL_AXES)
    n_plane = lax.axis_size(PLANE_AXES)
    rows, width = features.shape
    per = rows // EDGE
    half_tiles = n_plane * per
    src = (
        (((src // per) % 2) ^ lax.axis_index("core")) * half_tiles
        + (src // (2 * per)) * per
        + src % per
    ).astype(jnp.int32)

    def tiled(value):
        return value.reshape(-1, EDGE, EDGE)

    received = []
    for chunk in range(2):
        part = features[:, chunk * EDGE : (chunk + 1) * EDGE]
        received.append(exchange(copies(part, n_plane), PLANE_AXES))
    terms = []
    for chunk in range(2):
        mine = received[chunk]
        other = swap_core(mine)
        (partial,) = spread(
            tiles, src, dest, count, [tiled(mine), tiled(other)], [n_row * per], False, f"forward{chunk}"
        )
        terms.append(exchange(partial.reshape(n_row, rows, EDGE), ROW_AXES))
    hidden, grad0, grad1, gathered, grad_pre = middle(terms[0], terms[1], weight, out_grad)

    received = [exchange(copies(grad, n_row), ROW_AXES) for grad in (grad0, grad1)]
    weight_term = pl.pallas_call(
        weight_body,
        out_shape=jax.ShapeDtypeStruct((width, width), jnp.float32),
        name="weight_term",
    )(gathered, grad_pre)
    pieces = exchange(weight_term.reshape(n_row, width // n_row, width), ROW_AXES)
    piece = jnp.sum(pieces, axis=0)
    pieces = exchange(copies(piece, n_col), COL_AXES)
    piece = jnp.sum(pieces, axis=0)
    grad_w = exchange(copies(piece, n_row), ROW_AXES).reshape(width, width)
    nodes = rows * n_row * n_col
    grad_w = grad_w * nodes ** (-0.5)

    grads = []
    for chunk in range(2):
        mine, other = spread(
            tiles,
            dest,
            src,
            count,
            [tiled(received[chunk])],
            [half_tiles, half_tiles],
            True,
            f"backward{chunk}",
        )
        share = mine + swap_core(other)
        arrived = exchange(share.reshape(n_plane, rows, EDGE), PLANE_AXES)
        grads.append(jnp.sum(arrived, axis=0))
    grad_x = jnp.concatenate(grads, axis=1)
    return hidden, grad_x, grad_w


def solution(mesh):
    chips = Mesh(mesh.devices.reshape(4, 2, 2, 4, 2), ROW_AXES + COL_AXES)
    placed = (
        P(ROW_AXES + COL_AXES, None),
        P(),
        P(COL_AXES, ROW_AXES, None, None, None),
        P(COL_AXES, ROW_AXES, None, None),
        P(COL_AXES, ROW_AXES),
        P(COL_AXES + ROW_AXES, None),
    )
    return jax.shard_map(
        body,
        mesh=chips,
        in_specs=placed,
        out_specs=(P(COL_AXES + ROW_AXES, None), P(ROW_AXES + COL_AXES, None), P()),
        check_vma=False,
    )
```

```python
import functools

import jax
import jax.numpy as jnp
from jax import lax
from jax.experimental import pallas as pl
from jax.experimental.pallas import tpu as pltpu
from jax.sharding import Mesh
from jax.sharding import PartitionSpec as P

EDGE = 128
GROUP = 64
UNROLL = 32
ROW_AXES = ("y", "xh")
COL_AXES = ("xl", "z", "core")
PLANE_AXES = ("xl", "z")
VMEM_LIMIT = 48 << 20


def split(value):
    high = value.astype(jnp.bfloat16)
    low = (value - high.astype(jnp.float32)).astype(jnp.bfloat16)
    return high, low


def dot3(left, right, dims=((1,), (0,))):
    dot = functools.partial(
        lax.dot_general, dimension_numbers=(dims, ((), ())), preferred_element_type=jnp.float32
    )
    left_high, left_low = split(left)
    right_high, right_low = split(right)
    return dot(left_high, right_high) + (dot(left_high, right_low) + dot(left_low, right_high))


def spread_body(flipped, n_src, take, put, count, tiles, *refs):
    sources, (outs, (paired, total)) = refs[:n_src], (refs[n_src:-2], refs[-2:])
    step = pl.program_id(0)

    @pl.when(step == 0)
    def _():
        total[...] = jnp.zeros_like(total)
        place = 0
        for source in sources:

            def pair(index, carry, source=source, place=place):
                high, low = split(source[pl.ds(pl.multiple_of(index * EDGE, EDGE), EDGE), :])
                paired[place + index, :EDGE, :EDGE] = high
                paired[place + index, :EDGE, EDGE:] = low
                paired[place + index, EDGE:, :EDGE] = high
                paired[place + index, EDGE:, EDGE:] = jnp.zeros_like(low)
                return carry

            lax.fori_loop(0, source.shape[0] // EDGE, pair, 0)
            place += source.shape[0] // EDGE

    first = step * GROUP

    def one(slot):
        tile = tiles[slot]
        high, low = split(tile.T if flipped else tile)
        both = jnp.dot(
            jnp.concatenate([high, low], axis=1),
            paired[take[first + slot]],
            preferred_element_type=jnp.float32,
        )
        where = put[first + slot]
        total[where] += both[:, :EDGE] + both[:, EDGE:]

    live = jnp.clip(count[0] - first, 0, GROUP)
    blocks = live // UNROLL

    def block(index, carry):
        for offset in range(UNROLL):
            one(index * UNROLL + offset)
        return carry

    def rest(slot, carry):
        one(slot)
        return carry

    lax.fori_loop(0, blocks, block, 0)
    lax.fori_loop(blocks * UNROLL, live, rest, 0)

    @pl.when(step == pl.num_programs(0) - 1)
    def _():
        place = 0
        for out in outs:
            out[...] = total[place : place + out.shape[0]]
            place += out.shape[0]


def spread(tiles, take, put, count, sources, rows, out_counts, flipped, name):
    slots = tiles.shape[0]
    src_count = len(sources) * rows // EDGE
    whole = lambda *unused: (0, 0, 0)
    return pl.pallas_call(
        functools.partial(spread_body, flipped, len(sources)),
        grid_spec=pltpu.PrefetchScalarGridSpec(
            num_scalar_prefetch=3,
            grid=(slots // GROUP,),
            in_specs=[
                pl.BlockSpec(
                    (GROUP, EDGE, EDGE),
                    lambda g, take, put, count: (jnp.minimum(g, (count[0] - 1) // GROUP), 0, 0),
                )
            ]
            + [pl.BlockSpec((rows, EDGE), lambda *unused: (0, 0)) for source in sources],
            out_specs=[pl.BlockSpec((n, EDGE, EDGE), whole) for n in out_counts],
            scratch_shapes=[
                pltpu.VMEM((src_count, 2 * EDGE, 2 * EDGE), jnp.bfloat16),
                pltpu.VMEM((sum(out_counts), EDGE, EDGE), jnp.float32),
            ],
        ),
        out_shape=[jax.ShapeDtypeStruct((n, EDGE, EDGE), jnp.float32) for n in out_counts],
        compiler_params=pltpu.CompilerParams(vmem_limit_bytes=VMEM_LIMIT),
        cost_estimate=pl.CostEstimate(
            flops=2 * slots * EDGE * 4 * EDGE * EDGE,
            bytes_accessed=slots * EDGE * EDGE * 4,
            transcendentals=0,
        ),
        name=name,
    )(take, put, count, tiles, *sources)


def whole_call(kernel, outs, *args, skipped=0, name):
    here, there = pl.BlockSpec(memory_space=pltpu.VMEM), pl.BlockSpec(memory_space=pl.ANY)
    return pl.pallas_call(
        kernel,
        in_specs=[here] * (len(args) - skipped) + [there] * skipped,
        out_specs=[here] * len(outs),
        out_shape=[jax.ShapeDtypeStruct(shape, jnp.float32) for shape in outs],
        compiler_params=pltpu.CompilerParams(vmem_limit_bytes=VMEM_LIMIT),
        name=name,
    )(*args)


def middle_body(terms0, terms1, weight, out_grad, hidden, grad0, grad1, gathered, grad_pre):
    parts = [jnp.sum(terms[...], axis=0) for terms in (terms0, terms1)]
    mixed = jnp.concatenate(parts, axis=1)
    gathered[...] = mixed
    pre_act = dot3(mixed, weight[...])
    sigma = jax.nn.sigmoid(pre_act)
    hidden[...] = pre_act * sigma
    slope = sigma * (1.0 + pre_act * (1.0 - sigma))
    local = out_grad[...] * slope
    grad_pre[...] = local
    back = dot3(local, weight[...], ((1,), (1,)))
    grad0[...] = back[:, :EDGE]
    grad1[...] = back[:, EDGE:]


def weight_body(gathered, grad_pre, out):
    term = dot3(gathered[...], grad_pre[...], ((0,), (0,)))
    me = lax.axis_index("xh")
    n_y, piece = out.shape[1], out.shape[2] // 2
    for place in range(n_y):
        for half in range(2):
            first = (place * 2 + half) * piece
            for side in range(2):
                out[half ^ me, place, side * piece : (side + 1) * piece, :] = term[
                    first : first + piece, side * EDGE : (side + 1) * EDGE
                ]


def pair_body(mine, other, *refs):
    out = refs[-1]
    rows = mine.shape[0]
    out[:rows] = mine[...]
    out[rows:] = other[...]


def ring_body(n_ring, grad, other, weight_part, *refs):
    outs = refs[-n_ring:]
    me = lax.axis_index("y")
    rows = grad.shape[0]
    piece = weight_part.shape[1]
    for step, out in enumerate(outs):
        out[:rows] = grad[...]
        out[rows : 2 * rows] = other[:rows]
        place = lax.rem(me + step, n_ring)
        out[2 * rows :] = weight_part[place] + other[pl.ds(rows + place * piece, piece), :]


def share_body(mine, other, piece, other_piece, out):
    rows = out.shape[1] - piece.shape[0]
    both = piece[...] + other_piece[...]
    for place in range(out.shape[0]):
        here = pl.ds(place * rows, rows)
        out[place, :rows] = mine[here, :] + other[here, :]
        out[place, rows:] = both


def add_body(mine, other, out):
    out[...] = mine[...] + other[...]


def sum_body(terms, grad, piece):
    total = jnp.sum(terms[...], axis=0)
    rows = grad.shape[0]
    grad[...] = total[:rows]
    piece[...] = total[rows:]


def finish_body(grad0, terms1, out):
    out[:, :EDGE] = grad0[...]
    out[:, EDGE:] = jnp.sum(terms1[...], axis=0)


def exchange(value, axes):
    return lax.all_to_all(value, axes, 0, 0, tiled=True)


def swap(value, axis):
    return lax.ppermute(value, axis, [(0, 1), (1, 0)])


def ring_send(value, axis, step):
    size = lax.axis_size(axis)
    return lax.ppermute(value, axis, [(place, (place + step) % size) for place in range(size)])


def offset_of(ring_index, pair_index, ring, pair):
    step = (lax.axis_index(ring) - ring_index) % lax.axis_size(ring)
    return step * 2 + (pair_index ^ lax.axis_index(pair))


def body(features, weight, tile_vals, tile_index, tile_count, out_grad):
    tiles = tile_vals[0, 0]
    dest = tile_index[0, 0, 0]
    src = tile_index[0, 0, 1]
    count = tile_count[0]
    n_row = lax.axis_size(ROW_AXES)
    n_col = lax.axis_size(COL_AXES)
    n_plane = lax.axis_size(PLANE_AXES)
    n_z = lax.axis_size("z")
    n_y = lax.axis_size("y")
    rows, width = features.shape
    per = rows // EDGE
    half_tiles = n_plane * per
    src_home, src_tile = src // per, src % per
    src_core = (src_home % 2) ^ lax.axis_index("core")
    src_plane = src_home // 2
    src_take = (
        src_core * half_tiles + offset_of(src_plane % n_z, src_plane // n_z, "z", "xl") * per + src_tile
    ).astype(jnp.int32)
    src_put = (src_core * half_tiles + src_plane * per + src_tile).astype(jnp.int32)
    dest_home, dest_tile = dest // per, dest % per
    dest_take = (offset_of(dest_home // 2, dest_home % 2, "y", "xh") * per + dest_tile).astype(jnp.int32)

    terms = []
    before = []
    for chunk in range(2):
        part = features[:, chunk * EDGE : (chunk + 1) * EDGE]
        (both,) = whole_call(
            pair_body,
            [(2 * rows, EDGE)],
            part,
            swap(part, "xl"),
            *before,
            skipped=len(before),
            name=f"pair{chunk}",
        )
        mine = [both] + [ring_send(both, "z", step) for step in (1, 3, 2)]
        before = mine[1:]
        mine = [mine[0], mine[1], mine[3], mine[2]]
        other = [swap(value, "core") for value in mine]
        (partial,) = spread(
            tiles, src_take, dest, count, mine + other, 2 * rows, [n_row * per], False, f"forward{chunk}"
        )
        terms.append(exchange(partial.reshape(n_row, rows, EDGE), ROW_AXES))
    half = (rows, EDGE)
    full = (rows, width)
    hidden, grad0, grad1, gathered, grad_pre = whole_call(
        middle_body, [full, half, half, full, full], *terms, weight, out_grad, name="middle"
    )

    (both,) = whole_call(pair_body, [(2 * rows, EDGE)], grad0, swap(grad0, "xh"), name="pair2")
    received = [both] + [ring_send(both, "y", step) for step in (1, 3, 2)]
    before = received[1:]
    received0 = [received[0], received[1], received[3], received[2]]
    piece_rows = 2 * width // n_row
    (weight_part,) = whole_call(
        weight_body, [(2, n_y, piece_rows, EDGE)], gathered, grad_pre, name="weight_term"
    )
    other = swap(jnp.concatenate([grad1, weight_part[1].reshape(-1, EDGE)], axis=0), "xh")
    sends = whole_call(
        functools.partial(ring_body, n_y),
        [(2 * rows + piece_rows, EDGE)] * n_y,
        grad1,
        other,
        weight_part[0],
        *before,
        skipped=len(before),
        name="ring",
    )
    received1 = [sends[0]] + [ring_send(sends[step], "y", step) for step in range(1, n_y)]
    piece = sum(value[2 * rows :] for value in received1)

    shares = []
    for chunk, received in enumerate((received0, received1)):
        mine, other = spread(
            tiles,
            dest_take,
            src_put,
            count,
            received,
            2 * rows,
            [half_tiles, half_tiles],
            True,
            f"backward{chunk}",
        )
        mine = mine.reshape(-1, EDGE)
        other = swap(other.reshape(-1, EDGE), "core")
        if chunk == 0:
            (share,) = whole_call(
                share_body,
                [(n_plane, rows + piece_rows, EDGE)],
                mine,
                other,
                piece,
                swap(piece, "core"),
                name="share0",
            )
        else:
            (share,) = whole_call(add_body, [(n_plane * rows, EDGE)], mine, other, name="share1")
            share = share.reshape(n_plane, rows, EDGE)
        shares.append(exchange(share, PLANE_AXES))
    grad_x0, piece = whole_call(sum_body, [half, (piece_rows, EDGE)], shares[0], name="sum0")
    pieces = lax.all_gather(piece, ROW_AXES, axis=0, tiled=False)
    grad_w = pieces.reshape(n_row, 2, piece_rows // 2, EDGE).transpose(0, 2, 1, 3).reshape(width, width)
    grad_w = grad_w * (rows * n_row * n_col) ** (-0.5)
    (grad_x,) = whole_call(finish_body, [full], grad_x0, shares[1], name="finish")
    return hidden, grad_x, grad_w


def solution(mesh):
    chips = Mesh(mesh.devices.reshape(4, 2, 2, 4, 2), ROW_AXES + COL_AXES)
    placed = (
        P(ROW_AXES + COL_AXES, None),
        P(),
        P(COL_AXES, ROW_AXES, None, None, None),
        P(COL_AXES, ROW_AXES, None, None),
        P(COL_AXES, ROW_AXES),
        P(COL_AXES + ROW_AXES, None),
    )
    return jax.shard_map(
        body,
        mesh=chips,
        in_specs=placed,
        out_specs=(P(COL_AXES + ROW_AXES, None), P(ROW_AXES + COL_AXES, None), P()),
        check_vma=False,
    )
```

```python
import functools

import jax
import jax.numpy as jnp
from jax import lax
from jax.experimental import pallas as pl
from jax.experimental.pallas import tpu as pltpu
from jax.sharding import Mesh
from jax.sharding import PartitionSpec as P

EDGE = 128
BLOCK = 32
ROW_AXES = ("y", "xh")
COL_AXES = ("xl", "z", "core")
PLANE_AXES = ("xl", "z")
VMEM_LIMIT = 40 << 20


def split(value):
    high = value.astype(jnp.bfloat16)
    low = (value - high.astype(jnp.float32)).astype(jnp.bfloat16)
    return high, low


def dot3(left, right, dims=((1,), (0,))):
    dot = functools.partial(
        lax.dot_general, dimension_numbers=(dims, ((), ())), preferred_element_type=jnp.float32
    )
    left_high, left_low = split(left)
    right_high, right_low = split(right)
    return dot(left_high, right_high) + (dot(left_high, right_low) + dot(left_low, right_high))


def spread_body(flipped, n_src, n_out, take, put, count, tiles, *refs):
    sources, outs = refs[:n_src], refs[-4 - n_out : -4]
    paired, total, held, arrived = refs[-4:]
    slots = held.shape[0]

    def fetch(index):
        here = pl.ds(index * BLOCK, BLOCK)
        return pltpu.make_async_copy(tiles.at[here], held.at[here], arrived.at[index])

    for index in range(slots // BLOCK):

        @pl.when(index * BLOCK < count[0])
        def _(index=index):
            fetch(index).start()

    total[...] = jnp.zeros_like(total)
    rows = paired.shape[0] // n_src
    for place, source in enumerate(sources):

        def pair(index, carry, source=source, first=place * rows):
            high, low = split(source[pl.ds(pl.multiple_of(index * EDGE, EDGE), EDGE), :])
            paired[first + index, :EDGE, :EDGE] = high
            paired[first + index, :EDGE, EDGE:] = low
            paired[first + index, EDGE:, :EDGE] = high
            paired[first + index, EDGE:, EDGE:] = jnp.zeros_like(low)
            return carry

        lax.fori_loop(0, rows, pair, 0)

    def block(index, masked):
        for offset in range(BLOCK):
            slot = index * BLOCK + offset
            tile = held[slot]
            if masked:
                tile = jnp.where(slot < count[0], tile, 0.0)
            high, low = split(tile.T if flipped else tile)
            both = jnp.dot(
                jnp.concatenate([high, low], axis=1),
                paired[take[slot]],
                preferred_element_type=jnp.float32,
            )
            total[put[slot]] += both[:, :EDGE] + both[:, EDGE:]

    def whole_block(index, carry):
        fetch(index).wait()
        block(index, False)
        return carry

    blocks = count[0] // BLOCK
    lax.fori_loop(0, blocks, whole_block, 0)

    @pl.when(blocks * BLOCK < count[0])
    def _():
        fetch(blocks).wait()
        block(blocks, True)

    place = 0
    for out in outs:
        for index in range(out.shape[0] // EDGE):
            out[index * EDGE : (index + 1) * EDGE] = total[place + index]
        place += out.shape[0] // EDGE


def spread(tiles, take, put, count, sources, rows, out_rows, flipped, after, name):
    slots = tiles.shape[0]
    src_count = len(sources) * rows // EDGE
    scalars, here = pl.BlockSpec(memory_space=pltpu.SMEM), pl.BlockSpec(memory_space=pltpu.VMEM)
    there = pl.BlockSpec(memory_space=pl.ANY)
    return pl.pallas_call(
        functools.partial(spread_body, flipped, len(sources), len(out_rows)),
        in_specs=[scalars] * 3 + [there] + [here] * len(sources) + [there] * len(after),
        out_specs=[here] * len(out_rows),
        scratch_shapes=[
            pltpu.VMEM((src_count, 2 * EDGE, 2 * EDGE), jnp.bfloat16),
            pltpu.VMEM((sum(out_rows) // EDGE, EDGE, EDGE), jnp.float32),
            pltpu.VMEM(tiles.shape, jnp.float32),
            pltpu.SemaphoreType.DMA((slots // BLOCK,)),
        ],
        out_shape=[jax.ShapeDtypeStruct((n, EDGE), jnp.float32) for n in out_rows],
        compiler_params=pltpu.CompilerParams(vmem_limit_bytes=VMEM_LIMIT),
        cost_estimate=pl.CostEstimate(
            flops=2 * slots * EDGE * 4 * EDGE * EDGE,
            bytes_accessed=slots * EDGE * EDGE * 4,
            transcendentals=0,
        ),
        name=name,
    )(take, put, count, tiles, *sources, *after)


def whole_call(kernel, outs, *args, skipped=0, name):
    here, there = pl.BlockSpec(memory_space=pltpu.VMEM), pl.BlockSpec(memory_space=pl.ANY)
    return pl.pallas_call(
        kernel,
        in_specs=[here] * (len(args) - skipped) + [there] * skipped,
        out_specs=[here] * len(outs),
        out_shape=[jax.ShapeDtypeStruct(shape, jnp.float32) for shape in outs],
        compiler_params=pltpu.CompilerParams(vmem_limit_bytes=VMEM_LIMIT),
        name=name,
    )(*args)


def added(terms):
    values = [term[...] for term in terms]
    while len(values) > 1:
        if len(values) % 2:
            values = [values[0] + values[1]] + values[2:]
        half = len(values) // 2
        values = [left + right for left, right in zip(values[:half], values[half:])] if half else values
    return values[0]


def middle_body(n_first, n_second, *refs):
    firsts, seconds, rest = refs[:n_first], refs[n_first : n_first + n_second], refs[n_first + n_second :]
    weight, out_grad, hidden, grad0, grad1, gathered, grad_pre = rest
    mixed = jnp.concatenate([added(firsts), added(seconds)], axis=1)
    gathered[...] = mixed
    pre_act = dot3(mixed, weight[...])
    sigma = jax.nn.sigmoid(pre_act)
    hidden[...] = pre_act * sigma
    slope = sigma * (1.0 + pre_act * (1.0 - sigma))
    local = out_grad[...] * slope
    grad_pre[...] = local
    back = dot3(local, weight[...], ((1,), (1,)))
    grad0[...] = back[:, :EDGE]
    grad1[...] = back[:, EDGE:]


def weight_body(gathered, grad_pre, out):
    term = dot3(gathered[...], grad_pre[...], ((0,), (0,)))
    me = lax.axis_index("xh")
    n_y, piece = out.shape[1], out.shape[2] // 2
    for place in range(n_y):
        for half in range(2):
            first = (place * 2 + half) * piece
            for side in range(2):
                out[half ^ me, place, side * piece : (side + 1) * piece, :] = term[
                    first : first + piece, side * EDGE : (side + 1) * EDGE
                ]


def pair_body(mine, other, *refs):
    out = refs[-1]
    rows = mine.shape[0]
    out[:rows] = mine[...]
    out[rows:] = other[...]


def ring_body(n_ring, grad, other, weight_part, *refs):
    outs = refs[-n_ring:]
    me = lax.axis_index("y")
    rows = grad.shape[0]
    piece = weight_part.shape[1]
    for step, out in enumerate(outs):
        out[:rows] = grad[...]
        out[rows : 2 * rows] = other[:rows]
        place = lax.rem(me + step, n_ring)
        out[2 * rows :] = weight_part[place] + other[pl.ds(rows + place * piece, piece), :]


def fold_body(n_terms, *refs):
    terms, (own, other) = refs[:n_terms], refs[n_terms:]
    total = added(terms)
    rows = own.shape[0]
    own[...] = total[:rows]
    other[...] = total[rows : 2 * rows]


def share_body(mine, other, piece, other_piece, *outs):
    rows = mine.shape[0] // len(outs)
    both = piece[...] + other_piece[...]
    for step, out in enumerate(outs):
        here = pl.ds(step * rows, rows)
        out[:rows] = mine[here, :] + other[here, :]
        out[rows:] = both


def fold_share_body(n_terms, *refs):
    terms, (own, other) = refs[:n_terms], refs[n_terms:]
    total = added(terms)
    rows = own.shape[0]
    own[...] = total[:rows]
    other[...] = total[rows:]


def add_body(mine, other, *outs):
    rows = mine.shape[0] // len(outs)
    for step, out in enumerate(outs):
        here = pl.ds(step * rows, rows)
        out[...] = mine[here, :] + other[here, :]


def finish_body(grad0, other0, *refs):
    terms, out = refs[:-1], refs[-1]
    out[:, :EDGE] = grad0[...] + other0[: grad0.shape[0]]
    out[:, EDGE:] = added(terms)


def assemble_body(scale, n_ring, own, other, out):
    count = own.shape[0] // (2 * n_ring)
    for step in range(n_ring):
        ring = lax.rem(lax.axis_index("y") + n_ring - step, n_ring)
        for half, pieces in enumerate((own, other)):
            first = (ring * 2 + (lax.axis_index("xh") ^ half)) * count
            here = pl.ds(pl.multiple_of(first, count), count)
            for side in range(2):
                place = (step * 2 + side) * count
                out[here, side * EDGE : (side + 1) * EDGE] = pieces[place : place + count, :] * scale


def swap(value, axis):
    return lax.ppermute(value, axis, [(0, 1), (1, 0)])


def ring_send(value, axis, step):
    size = lax.axis_size(axis)
    return lax.ppermute(value, axis, [(place, (place + step) % size) for place in range(size)])


def offset_send(value, axes, ring, offset):
    sizes = [lax.axis_size(axis) for axis in axes]
    hops = []
    for a in range(sizes[0]):
        for b in range(sizes[1]):
            if axes[0] == ring:
                to = (a + offset // 2) % sizes[0], b ^ (offset % 2)
            else:
                to = a ^ (offset % 2), (b + offset // 2) % sizes[1]
            hops.append((a * sizes[1] + b, to[0] * sizes[1] + to[1]))
    return lax.ppermute(value, axes, hops)


def offset_of(ring_index, pair_index, ring, pair, sign):
    step = (sign * (lax.axis_index(ring) - ring_index)) % lax.axis_size(ring)
    return step * 2 + (pair_index ^ lax.axis_index(pair))


def body(features, weight, tile_vals, tile_index, tile_count, out_grad):
    tiles = tile_vals[0, 0]
    dest = tile_index[0, 0, 0]
    src = tile_index[0, 0, 1]
    count = tile_count[0]
    n_row = lax.axis_size(ROW_AXES)
    n_col = lax.axis_size(COL_AXES)
    n_plane = lax.axis_size(PLANE_AXES)
    n_z = lax.axis_size("z")
    n_y = lax.axis_size("y")
    rows, width = features.shape
    per = rows // EDGE
    half_tiles = n_plane * per
    src_home, src_tile = src // per, src % per
    src_half = ((src_home % 2) ^ lax.axis_index("core")) * half_tiles + src_tile
    dest_home, dest_tile = dest // per, dest % per

    def src_place(sign):
        plane = src_home // 2
        return src_half + per * offset_of(plane % n_z, plane // n_z, "z", "xl", sign)

    def dest_place(sign):
        return dest_tile + per * offset_of(dest_home // 2, dest_home % 2, "y", "xh", sign)

    live = jnp.arange(tiles.shape[0], dtype=jnp.int32) < count[0]
    src_take, dest_put, dest_take, src_put = [
        jnp.where(live, index, 0).astype(jnp.int32)
        for index in (src_place(1), dest_place(-1), dest_place(1), src_place(-1))
    ]

    half = (rows, EDGE)
    full = (rows, width)
    terms = []
    before = []
    for chunk in range(2):
        part = features[:, chunk * EDGE : (chunk + 1) * EDGE]
        (both,) = whole_call(
            pair_body,
            [(2 * rows, EDGE)],
            part,
            swap(part, "xl"),
            *before,
            skipped=len(before),
            name=f"pair{chunk}",
        )
        mine = [both] + [ring_send(both, "z", step) for step in range(1, 4)]
        before = mine[1:]
        other = [swap(value, "core") for value in mine]
        partials = spread(
            tiles,
            src_take,
            dest_put,
            count,
            mine + other,
            2 * rows,
            [2 * rows] * n_y if chunk == 0 else [rows] * n_row,
            False,
            [],
            f"forward{chunk}",
        )
        if chunk == 0:
            arrived = [ring_send(partials[step], "y", step) for step in range(1, 4)]
            own, other = whole_call(
                functools.partial(fold_body, n_y), [half, half], partials[0], *arrived, name="fold0"
            )
            terms.append([own, swap(other, "xh")])
        else:
            terms.append(
                [partials[0]]
                + [offset_send(partials[offset], ROW_AXES, "y", offset) for offset in range(1, n_row)]
            )
    hidden, grad0, grad1, gathered, grad_pre = whole_call(
        functools.partial(middle_body, len(terms[0]), len(terms[1])),
        [full, half, half, full, full],
        *terms[0],
        *terms[1],
        weight,
        out_grad,
        name="middle",
    )

    (both,) = whole_call(pair_body, [(2 * rows, EDGE)], grad0, swap(grad0, "xh"), name="pair2")
    received = [both] + [ring_send(both, "y", step) for step in range(1, 4)]
    received0 = received
    piece_rows = 2 * width // n_row
    (weight_part,) = whole_call(
        weight_body, [(2, n_y, piece_rows, EDGE)], gathered, grad_pre, name="weight_term"
    )
    other = swap(jnp.concatenate([grad1, weight_part[1].reshape(-1, EDGE)], axis=0), "xh")
    sends = whole_call(
        functools.partial(ring_body, n_y),
        [(2 * rows + piece_rows, EDGE)] * n_y,
        grad1,
        other,
        weight_part[0],
        name="ring",
    )
    received1 = [sends[0]] + [ring_send(sends[step], "y", step) for step in range(1, n_y)]
    piece = sum(value[2 * rows :] for value in received1)

    for chunk, received in enumerate((received0, received1)):
        mine, other = spread(
            tiles,
            dest_take,
            src_put,
            count,
            received,
            2 * rows,
            [half_tiles * EDGE] * 2,
            True,
            sends[1:2] if chunk == 0 else [],
            f"backward{chunk}",
        )
        other = swap(other, "core")
        if chunk == 0:
            shares = whole_call(
                share_body,
                [(2 * rows + piece_rows, EDGE)] * n_z,
                mine,
                other,
                piece,
                swap(piece, "core"),
                name="share0",
            )
            arrived = [ring_send(shares[step], "z", step) for step in range(1, 4)]
            grad_x0, other0 = whole_call(
                functools.partial(fold_share_body, n_z),
                [half, (rows + piece_rows, EDGE)],
                shares[0],
                *arrived,
                name="fold1",
            )
            arrived0 = swap(other0, "xl")
        else:
            shares = whole_call(add_body, [half] * n_plane, mine, other, name="share1")
            arrived = [
                offset_send(shares[offset], PLANE_AXES, "z", offset) for offset in range(1, n_plane)
            ]
            (grad_x,) = whole_call(
                finish_body, [full], grad_x0, arrived0, shares[0], *arrived, name="finish"
            )
    piece = other0[rows:] + arrived0[rows:]
    pieces = [piece] + [ring_send(piece, "y", step) for step in range(1, 4)]
    pieces = jnp.concatenate(pieces, axis=0)
    scale = (rows * n_row * n_col) ** (-0.5)
    (grad_w,) = whole_call(
        functools.partial(assemble_body, scale, n_y),
        [(width, width)],
        pieces,
        swap(pieces, "xh"),
        name="assemble",
    )
    return hidden, grad_x, grad_w


def solution(mesh):
    chips = Mesh(mesh.devices.reshape(4, 2, 2, 4, 2), ROW_AXES + COL_AXES)
    placed = (
        P(ROW_AXES + COL_AXES, None),
        P(),
        P(COL_AXES, ROW_AXES, None, None, None),
        P(COL_AXES, ROW_AXES, None, None),
        P(COL_AXES, ROW_AXES),
        P(COL_AXES + ROW_AXES, None),
    )
    return jax.shard_map(
        body,
        mesh=chips,
        in_specs=placed,
        out_specs=(P(COL_AXES + ROW_AXES, None), P(ROW_AXES + COL_AXES, None), P()),
        check_vma=False,
    )
```

```python
import functools

import jax
import jax.numpy as jnp
from jax import lax
from jax.experimental import pallas as pl
from jax.experimental.pallas import tpu as pltpu
from jax.sharding import Mesh
from jax.sharding import PartitionSpec as P

EDGE = 128
BLOCK = 32
ROW_AXES = ("y", "xh")
COL_AXES = ("xl", "z", "core")
PLANE_AXES = ("xl", "z")
VMEM_LIMIT = 40 << 20


def split(value):
    high = value.astype(jnp.bfloat16)
    low = (value - high.astype(jnp.float32)).astype(jnp.bfloat16)
    return high, low


def dot3(left, right, dims=((1,), (0,))):
    dot = functools.partial(
        lax.dot_general, dimension_numbers=(dims, ((), ())), preferred_element_type=jnp.float32
    )
    left_high, left_low = split(left)
    right_high, right_low = split(right)
    return dot(left_high, right_high) + (dot(left_high, right_low) + dot(left_low, right_high))


def spread_body(flipped, n_src, n_out, take, put, count, tiles, *refs):
    sources, outs = refs[:n_src], refs[-4 - n_out : -4]
    paired, total, held, arrived = refs[-4:]
    slots = held.shape[0]

    def fetch(index):
        here = pl.ds(index * BLOCK, BLOCK)
        return pltpu.make_async_copy(tiles.at[here], held.at[here], arrived.at[index])

    for index in range(slots // BLOCK):

        @pl.when(index * BLOCK < count[0])
        def _(index=index):
            fetch(index).start()

    total[...] = jnp.zeros_like(total)
    first = 0
    for source in sources:
        rows = source.shape[0] // EDGE

        def pair(index, carry, source=source, first=first):
            high, low = split(source[pl.ds(pl.multiple_of(index * EDGE, EDGE), EDGE), :])
            paired[first + index, :EDGE, :EDGE] = high
            paired[first + index, :EDGE, EDGE:] = low
            paired[first + index, EDGE:, :EDGE] = high
            paired[first + index, EDGE:, EDGE:] = jnp.zeros_like(low)
            return carry

        lax.fori_loop(0, rows, pair, 0)
        first += rows

    def block(index, masked):
        for offset in range(BLOCK):
            slot = index * BLOCK + offset
            tile = held[slot]
            if masked:
                tile = jnp.where(slot < count[0], tile, 0.0)
            high, low = split(tile.T if flipped else tile)
            both = jnp.dot(
                jnp.concatenate([high, low], axis=1),
                paired[take[slot]],
                preferred_element_type=jnp.float32,
            )
            total[put[slot]] += both[:, :EDGE] + both[:, EDGE:]

    def whole_block(index, carry):
        fetch(index).wait()
        block(index, False)
        return carry

    blocks = count[0] // BLOCK
    lax.fori_loop(0, blocks, whole_block, 0)

    @pl.when(blocks * BLOCK < count[0])
    def _():
        fetch(blocks).wait()
        block(blocks, True)

    place = 0
    for out in outs:
        for index in range(out.shape[0] // EDGE):
            out[index * EDGE : (index + 1) * EDGE] = total[place + index]
        place += out.shape[0] // EDGE


def spread(tiles, take, put, count, sources, out_rows, flipped, after, name):
    slots = tiles.shape[0]
    src_count = sum(source.shape[0] // EDGE for source in sources)
    scalars, here = pl.BlockSpec(memory_space=pltpu.SMEM), pl.BlockSpec(memory_space=pltpu.VMEM)
    there = pl.BlockSpec(memory_space=pl.ANY)
    return pl.pallas_call(
        functools.partial(spread_body, flipped, len(sources), len(out_rows)),
        in_specs=[scalars] * 3 + [there] + [here] * len(sources) + [there] * len(after),
        out_specs=[here] * len(out_rows),
        scratch_shapes=[
            pltpu.VMEM((src_count, 2 * EDGE, 2 * EDGE), jnp.bfloat16),
            pltpu.VMEM((sum(out_rows) // EDGE, EDGE, EDGE), jnp.float32),
            pltpu.VMEM(tiles.shape, jnp.float32),
            pltpu.SemaphoreType.DMA((slots // BLOCK,)),
        ],
        out_shape=[jax.ShapeDtypeStruct((n, EDGE), jnp.float32) for n in out_rows],
        compiler_params=pltpu.CompilerParams(vmem_limit_bytes=VMEM_LIMIT),
        cost_estimate=pl.CostEstimate(flops=0, bytes_accessed=0, transcendentals=0),
        name=name,
    )(take, put, count, tiles, *sources, *after)


def whole_call(kernel, outs, *args, skipped=0, name):
    here, there = pl.BlockSpec(memory_space=pltpu.VMEM), pl.BlockSpec(memory_space=pl.ANY)
    return pl.pallas_call(
        kernel,
        in_specs=[here] * (len(args) - skipped) + [there] * skipped,
        out_specs=[here] * len(outs),
        out_shape=[jax.ShapeDtypeStruct(shape, jnp.float32) for shape in outs],
        compiler_params=pltpu.CompilerParams(vmem_limit_bytes=VMEM_LIMIT),
        name=name,
    )(*args)


def added(terms):
    return functools.reduce(lambda left, right: left + right, [term[...] for term in terms])


def middle_body(weight, out_grad, own, other, *refs):
    terms, (hidden, grad0, grad1, weight_part) = refs[:-4], refs[-4:]
    mixed = jnp.concatenate([own[...] + other[...], added(terms)], axis=1)
    pre_act = dot3(mixed, weight[...])
    sigma = jax.nn.sigmoid(pre_act)
    hidden[...] = pre_act * sigma
    slope = sigma * (1.0 + pre_act * (1.0 - sigma))
    local = out_grad[...] * slope
    back = dot3(local, weight[...], ((1,), (1,)))
    grad0[...] = back[:, :EDGE]
    grad1[...] = back[:, EDGE:]
    term = dot3(mixed, local, ((0,), (0,)))
    count = weight_part.shape[1] // 2
    for place in range(weight_part.shape[0]):
        for side in range(2):
            weight_part[place, side * count : (side + 1) * count, :] = term[
                place * count : (place + 1) * count, side * EDGE : (side + 1) * EDGE
            ]


def copies_body(value, *refs):
    out = refs[-1]
    rows = value.shape[0]
    for place in range(out.shape[0]):
        out[place, :rows] = value[...]
        if out.shape[1] > rows:
            out[place, rows:] = refs[0][place]


def unpack_body(arrived, rows_out, piece):
    rows = rows_out.shape[0] // arrived.shape[0]
    for place in range(arrived.shape[0]):
        rows_out[place * rows : (place + 1) * rows] = arrived[place, :rows]
    piece[...] = jnp.sum(arrived[:, rows:], axis=0)


def join_body(*refs):
    blocks, out = refs[:-2], refs[-1]
    rows = blocks[0].shape[0]
    for place, block in enumerate(blocks):
        out[place * rows : (place + 1) * rows] = block[...]


def pair_body(mine, other, *refs):
    out = refs[-1]
    rows = mine.shape[0]
    out[:rows] = mine[...]
    out[rows:] = other[...]


def fold_body(n_terms, *refs):
    terms, outs = refs[:n_terms], refs[n_terms + 1 :]
    total = added(terms)
    first = 0
    for out in outs:
        out[...] = total[first : first + out.shape[0]]
        first += out.shape[0]


def add_body(mine, other, *outs):
    rows = mine.shape[0] // len(outs)
    for step, out in enumerate(outs):
        here = pl.ds(step * rows, rows)
        out[...] = mine[here, :] + other[here, :]


def share_body(mine, other, piece, other_piece, out):
    rows = out.shape[1] - piece.shape[0]
    both = piece[...] + other_piece[...]
    for place in range(out.shape[0]):
        here = pl.ds(place * rows, rows)
        out[place, :rows] = mine[here, :] + other[here, :]
        out[place, rows:] = both


def sum_body(terms, grad, piece):
    total = jnp.sum(terms[...], axis=0)
    rows = grad.shape[0]
    grad[...] = total[:rows]
    piece[...] = total[rows:]


def finish_body(grad0, *refs):
    terms, out = refs[:-1], refs[-1]
    out[:, :EDGE] = grad0[...]
    out[:, EDGE:] = added(terms)


def assemble_body(scale, pieces, out):
    count = pieces.shape[1] // 2
    for place in range(pieces.shape[0]):
        for side in range(2):
            out[place * count : (place + 1) * count, side * EDGE : (side + 1) * EDGE] = (
                pieces[place, side * count : (side + 1) * count, :] * scale
            )


def swap(value, axis):
    return lax.ppermute(value, axis, [(0, 1), (1, 0)])


def ring_send(value, axis, step):
    size = lax.axis_size(axis)
    return lax.ppermute(value, axis, [(place, (place + step) % size) for place in range(size)])


def offset_send(value, axes, ring, offset):
    sizes = [lax.axis_size(axis) for axis in axes]
    hops = []
    for a in range(sizes[0]):
        for b in range(sizes[1]):
            if axes[0] == ring:
                to = (a + offset // 2) % sizes[0], b ^ (offset % 2)
            else:
                to = a ^ (offset % 2), (b + offset // 2) % sizes[1]
            hops.append((a * sizes[1] + b, to[0] * sizes[1] + to[1]))
    return lax.ppermute(value, axes, hops)


def exchange(value, axes):
    return lax.all_to_all(value, axes, 0, 0, tiled=True)


def offset_of(ring_index, pair_index, ring, pair, sign):
    step = (sign * (lax.axis_index(ring) - ring_index)) % lax.axis_size(ring)
    return step * 2 + (pair_index ^ lax.axis_index(pair))


def body(features, weight, tile_vals, tile_index, tile_count, out_grad):
    tiles = tile_vals[0, 0]
    dest = tile_index[0, 0, 0]
    src = tile_index[0, 0, 1]
    count = tile_count[0]
    n_row = lax.axis_size(ROW_AXES)
    n_col = lax.axis_size(COL_AXES)
    n_plane = lax.axis_size(PLANE_AXES)
    n_z = lax.axis_size("z")
    n_y = lax.axis_size("y")
    rows, width = features.shape
    per = rows // EDGE
    half_tiles = n_plane * per
    src_home, src_tile = src // per, src % per
    src_half = ((src_home % 2) ^ lax.axis_index("core")) * half_tiles + src_tile
    dest_home, dest_tile = dest // per, dest % per

    plane = src_home // 2

    def src_place(sign):
        return src_half + per * offset_of(plane % n_z, plane // n_z, "z", "xl", sign)

    def dest_place(sign):
        return dest_tile + per * offset_of(dest_home // 2, dest_home % 2, "y", "xh", sign)

    live = jnp.arange(tiles.shape[0], dtype=jnp.int32) < count[0]
    src_take, dest_put, dest_take0, dest_take1, src_put0, src_put1 = [
        jnp.where(live, index, 0).astype(jnp.int32)
        for index in (
            src_place(1),
            dest_place(-1),
            dest_place(1),
            dest,
            src_half + per * plane,
            src_place(-1),
        )
    ]

    half = (rows, EDGE)
    full = (rows, width)
    gathered = []
    for chunk in range(2):
        part = features[:, chunk * EDGE : (chunk + 1) * EDGE]
        after = gathered[0][1:] if chunk else []
        (both,) = whole_call(
            pair_body,
            [(2 * rows, EDGE)],
            part,
            swap(part, "xl"),
            *after,
            skipped=len(after),
            name=f"pair{chunk}",
        )
        gathered.append([both] + [ring_send(both, "z", step) for step in range(1, n_z)])
    partial0 = spread(
        tiles,
        src_take,
        dest_put,
        count,
        gathered[0] + [swap(block, "core") for block in gathered[0]],
        [2 * rows] * n_y,
        False,
        [],
        "forward0",
    )
    (joined,) = whole_call(
        join_body, [(half_tiles * EDGE, EDGE)], *gathered[1], partial0[0], skipped=1, name="join"
    )
    partial1 = spread(
        tiles,
        src_take,
        dest_put,
        count,
        [joined, swap(joined, "core")],
        [rows] * n_row,
        False,
        [],
        "forward1",
    )
    arrived = [offset_send(partial1[offset], ROW_AXES, "y", offset) for offset in range(1, n_row)]
    arrived0 = [ring_send(partial0[step], "y", step) for step in range(1, n_y)]
    own, other = whole_call(
        functools.partial(fold_body, n_y),
        [half, half],
        partial0[0],
        *arrived0,
        arrived[0],
        skipped=1,
        name="fold0",
    )
    piece_rows = 2 * width // n_row
    hidden, grad0, grad1, weight_part = whole_call(
        middle_body,
        [full, half, half, (n_row, piece_rows, EDGE)],
        weight,
        out_grad,
        own,
        swap(other, "xh"),
        partial1[0],
        *arrived,
        name="middle",
    )

    (both,) = whole_call(pair_body, [(2 * rows, EDGE)], grad0, swap(grad0, "xh"), name="pair2")
    sources0 = [both] + [ring_send(both, "y", step) for step in range(1, n_y)]
    (copied,) = whole_call(
        copies_body, [(n_row, rows + piece_rows, EDGE)], grad1, weight_part, both, skipped=1, name="copies"
    )
    arrived = exchange(copied, ROW_AXES)
    sources1, piece = whole_call(
        unpack_body, [(n_row * rows, EDGE), (piece_rows, EDGE)], arrived, name="unpack"
    )
    mine, other = spread(
        tiles,
        dest_take0,
        src_put0,
        count,
        sources0,
        [half_tiles * EDGE] * 2,
        True,
        [copied],
        "backward0",
    )
    (share,) = whole_call(
        share_body,
        [(n_plane, rows + piece_rows, EDGE)],
        mine,
        swap(other, "core"),
        piece,
        swap(piece, "core"),
        name="share0",
    )
    terms = exchange(share, PLANE_AXES)
    mine, other = spread(
        tiles,
        dest_take1,
        src_put1,
        count,
        [sources1],
        [half_tiles * EDGE] * 2,
        True,
        [share],
        "backward1",
    )
    shares = whole_call(add_body, [half] * n_plane, mine, swap(other, "core"), name="share1")
    arrived = [offset_send(shares[offset], PLANE_AXES, "z", offset) for offset in range(1, n_plane)]
    grad_x0, piece = whole_call(sum_body, [half, (piece_rows, EDGE)], terms, name="sum0")
    (grad_x,) = whole_call(finish_body, [full], grad_x0, shares[0], *arrived, name="finish")

    pieces = exchange(jnp.broadcast_to(piece[None], (n_row, piece_rows, EDGE)), ROW_AXES)
    scale = (rows * n_row * n_col) ** (-0.5)
    (grad_w,) = whole_call(functools.partial(assemble_body, scale), [full], pieces, name="assemble")
    return hidden, grad_x, grad_w


def solution(mesh):
    chips = Mesh(mesh.devices.reshape(4, 2, 2, 4, 2), ROW_AXES + COL_AXES)
    placed = (
        P(ROW_AXES + COL_AXES, None),
        P(),
        P(COL_AXES, ROW_AXES, None, None, None),
        P(COL_AXES, ROW_AXES, None, None),
        P(COL_AXES, ROW_AXES),
        P(COL_AXES + ROW_AXES, None),
    )
    return jax.shard_map(
        body,
        mesh=chips,
        in_specs=placed,
        out_specs=(P(COL_AXES + ROW_AXES, None), P(ROW_AXES + COL_AXES, None), P()),
        check_vma=False,
    )
```

```python
import functools

import jax
import jax.numpy as jnp
from jax import lax
from jax.experimental import pallas as pl
from jax.experimental.pallas import tpu as pltpu
from jax.sharding import Mesh
from jax.sharding import PartitionSpec as P

EDGE = 128
BLOCK = 32
ROW_AXES = ("y", "xh")
COL_AXES = ("xl", "z", "core")
PLANE_AXES = ("xl", "z")
VMEM_LIMIT = 40 << 20


def split(value):
    high = value.astype(jnp.bfloat16)
    low = (value - high.astype(jnp.float32)).astype(jnp.bfloat16)
    return high, low


def dot3(left, right, dims=((1,), (0,))):
    dot = functools.partial(
        lax.dot_general, dimension_numbers=(dims, ((), ())), preferred_element_type=jnp.float32
    )
    left_high, left_low = split(left)
    right_high, right_low = split(right)
    return dot(left_high, right_high) + (dot(left_high, right_low) + dot(left_low, right_high))


def spread_body(flipped, n_src, n_out, take, put, count, tiles, *refs):
    sources, outs = refs[:n_src], refs[-4 - n_out : -4]
    paired, total, held, arrived = refs[-4:]
    slots = held.shape[0]

    def fetch(index):
        here = pl.ds(index * BLOCK, BLOCK)
        return pltpu.make_async_copy(tiles.at[here], held.at[here], arrived.at[index])

    for index in range(slots // BLOCK):

        @pl.when(index * BLOCK < count[0])
        def _(index=index):
            fetch(index).start()

    total[...] = jnp.zeros_like(total)
    first = 0
    for source in sources:
        rows = source.shape[0] // EDGE

        def pair(index, carry, source=source, first=first):
            high, low = split(source[pl.ds(pl.multiple_of(index * EDGE, EDGE), EDGE), :])
            paired[first + index, :EDGE, :EDGE] = high
            paired[first + index, :EDGE, EDGE:] = low
            paired[first + index, EDGE:, :EDGE] = high
            paired[first + index, EDGE:, EDGE:] = jnp.zeros_like(low)
            return carry

        lax.fori_loop(0, rows, pair, 0)
        first += rows

    def block(index, masked):
        for offset in range(BLOCK):
            slot = index * BLOCK + offset
            tile = held[slot]
            if masked:
                tile = jnp.where(slot < count[0], tile, 0.0)
            high, low = split(tile.T if flipped else tile)
            both = jnp.dot(
                jnp.concatenate([high, low], axis=1),
                paired[take[slot]],
                preferred_element_type=jnp.float32,
            )
            total[put[slot]] += both[:, :EDGE] + both[:, EDGE:]

    def whole_block(index, carry):
        fetch(index).wait()
        block(index, False)
        return carry

    blocks = count[0] // BLOCK
    lax.fori_loop(0, blocks, whole_block, 0)

    @pl.when(blocks * BLOCK < count[0])
    def _():
        fetch(blocks).wait()
        block(blocks, True)

    place = 0
    for out in outs:
        for index in range(out.shape[0] // EDGE):
            out[index * EDGE : (index + 1) * EDGE] = total[place + index]
        place += out.shape[0] // EDGE


def spread(tiles, take, put, count, sources, out_rows, flipped, after, name):
    slots = tiles.shape[0]
    src_count = sum(source.shape[0] // EDGE for source in sources)
    scalars, here = pl.BlockSpec(memory_space=pltpu.SMEM), pl.BlockSpec(memory_space=pltpu.VMEM)
    there = pl.BlockSpec(memory_space=pl.ANY)
    return pl.pallas_call(
        functools.partial(spread_body, flipped, len(sources), len(out_rows)),
        in_specs=[scalars] * 3 + [there] + [here] * len(sources) + [there] * len(after),
        out_specs=[here] * len(out_rows),
        scratch_shapes=[
            pltpu.VMEM((src_count, 2 * EDGE, 2 * EDGE), jnp.bfloat16),
            pltpu.VMEM((sum(out_rows) // EDGE, EDGE, EDGE), jnp.float32),
            pltpu.VMEM(tiles.shape, jnp.float32),
            pltpu.SemaphoreType.DMA((slots // BLOCK,)),
        ],
        out_shape=[jax.ShapeDtypeStruct((n, EDGE), jnp.float32) for n in out_rows],
        compiler_params=pltpu.CompilerParams(vmem_limit_bytes=VMEM_LIMIT),
        cost_estimate=pl.CostEstimate(flops=0, bytes_accessed=0, transcendentals=0),
        name=name,
    )(take, put, count, tiles, *sources, *after)


def whole_call(kernel, outs, *args, skipped=0, name):
    here, there = pl.BlockSpec(memory_space=pltpu.VMEM), pl.BlockSpec(memory_space=pl.ANY)
    return pl.pallas_call(
        kernel,
        in_specs=[here] * (len(args) - skipped) + [there] * skipped,
        out_specs=[here] * len(outs),
        out_shape=[jax.ShapeDtypeStruct(shape, jnp.float32) for shape in outs],
        compiler_params=pltpu.CompilerParams(vmem_limit_bytes=VMEM_LIMIT),
        name=name,
    )(*args)


def added(terms):
    return functools.reduce(lambda left, right: left + right, [term[...] for term in terms])


def middle_body(weight, out_grad, own, other, *refs):
    terms, (hidden, grad0, grad1, weight_part) = refs[:-4], refs[-4:]
    mixed = jnp.concatenate([own[...] + other[...], added(terms)], axis=1)
    pre_act = dot3(mixed, weight[...])
    sigma = jax.nn.sigmoid(pre_act)
    hidden[...] = pre_act * sigma
    slope = sigma * (1.0 + pre_act * (1.0 - sigma))
    local = out_grad[...] * slope
    back = dot3(local, weight[...], ((1,), (1,)))
    grad0[...] = back[:, :EDGE]
    grad1[...] = back[:, EDGE:]
    term = dot3(mixed, local, ((0,), (0,)))
    count = weight_part.shape[1] // 2
    for place in range(weight_part.shape[0]):
        for side in range(2):
            weight_part[place, side * count : (side + 1) * count, :] = term[
                place * count : (place + 1) * count, side * EDGE : (side + 1) * EDGE
            ]


def copies_body(value, *refs):
    out = refs[-1]
    rows = value.shape[0]
    for place in range(out.shape[0]):
        out[place, :rows] = value[...]
        if out.shape[1] > rows:
            out[place, rows:] = refs[0][place]


def unpack_body(arrived, rows_out, piece):
    rows = rows_out.shape[0] // arrived.shape[0]
    for place in range(arrived.shape[0]):
        rows_out[place * rows : (place + 1) * rows] = arrived[place, :rows]
    piece[...] = jnp.sum(arrived[:, rows:], axis=0)


def join_body(*refs):
    blocks, out = refs[:-1], refs[-1]
    rows = blocks[0].shape[0]
    for place, block in enumerate(blocks):
        out[place * rows : (place + 1) * rows] = block[...]


def join_pairs_body(*refs):
    blocks, out = refs[:-2], refs[-1]
    rows = blocks[0].shape[0] // 2
    for place, block in enumerate(blocks):
        for half in range(2):
            first = (half * len(blocks) + place) * rows
            out[first : first + rows] = block[half * rows : (half + 1) * rows]


def pair_body(mine, other, *refs):
    out = refs[-1]
    rows = mine.shape[0]
    out[:rows] = mine[...]
    out[rows:] = other[...]


def fold_body(n_terms, *refs):
    terms, outs = refs[:n_terms], refs[n_terms + 1 :]
    total = added(terms)
    first = 0
    for out in outs:
        out[...] = total[first : first + out.shape[0]]
        first += out.shape[0]


def add_body(place, count, mine, other, *refs):
    for step, out in enumerate(refs[-count:]):
        here = pl.ds((place + step) * out.shape[0], out.shape[0])
        out[...] = mine[here, :] + other[here, :]


def share_body(mine, other, piece, other_piece, out):
    rows = out.shape[1] - piece.shape[0]
    both = piece[...] + other_piece[...]
    for place in range(out.shape[0]):
        here = pl.ds(place * rows, rows)
        out[place, :rows] = mine[here, :] + other[here, :]
        out[place, rows:] = both


def sum_body(terms, grad, piece):
    total = jnp.sum(terms[...], axis=0)
    rows = grad.shape[0]
    grad[...] = total[:rows]
    piece[...] = total[rows:]


def finish_body(grad0, *refs):
    terms, out = refs[:-1], refs[-1]
    out[:, :EDGE] = grad0[...]
    out[:, EDGE:] = added(terms)


def assemble_body(scale, pieces, out):
    count = pieces.shape[1] // 2
    for place in range(pieces.shape[0]):
        for side in range(2):
            out[place * count : (place + 1) * count, side * EDGE : (side + 1) * EDGE] = (
                pieces[place, side * count : (side + 1) * count, :] * scale
            )


def swap(value, axis):
    return lax.ppermute(value, axis, [(0, 1), (1, 0)])


def ring_send(value, axis, step):
    size = lax.axis_size(axis)
    return lax.ppermute(value, axis, [(place, (place + step) % size) for place in range(size)])


def offset_send(value, axes, ring, offset):
    sizes = [lax.axis_size(axis) for axis in axes]
    hops = []
    for a in range(sizes[0]):
        for b in range(sizes[1]):
            if axes[0] == ring:
                to = (a + offset // 2) % sizes[0], b ^ (offset % 2)
            else:
                to = a ^ (offset % 2), (b + offset // 2) % sizes[1]
            hops.append((a * sizes[1] + b, to[0] * sizes[1] + to[1]))
    return lax.ppermute(value, axes, hops)


def exchange(value, axes):
    return lax.all_to_all(value, axes, 0, 0, tiled=True)


def gather_place(ring_index, pair_index, ring, pair):
    size = lax.axis_size(ring)
    return (pair_index ^ lax.axis_index(pair)) * size + (lax.axis_index(ring) - ring_index) % size


def scatter_place(ring_index, pair_index, ring, pair):
    step = (ring_index - lax.axis_index(ring)) % lax.axis_size(ring)
    return step * 2 + (pair_index ^ lax.axis_index(pair))


def around(value, axis):
    return [value] + [ring_send(value, axis, step) for step in range(1, lax.axis_size(axis))]


def body(features, weight, tile_vals, tile_index, tile_count, out_grad):
    tiles = tile_vals[0, 0]
    dest = tile_index[0, 0, 0]
    src = tile_index[0, 0, 1]
    count = tile_count[0]
    n_row = lax.axis_size(ROW_AXES)
    n_col = lax.axis_size(COL_AXES)
    n_plane = lax.axis_size(PLANE_AXES)
    n_z = lax.axis_size("z")
    n_y = lax.axis_size("y")
    rows, width = features.shape
    per = rows // EDGE
    half_tiles = n_plane * per
    src_home, src_tile = src // per, src % per
    src_half = ((src_home % 2) ^ lax.axis_index("core")) * half_tiles + src_tile
    dest_home, dest_tile = dest // per, dest % per

    plane = src_home // 2

    src_at = (plane % n_z, plane // n_z, "z", "xl")
    dest_at = (dest_home // 2, dest_home % 2, "y", "xh")

    live = jnp.arange(tiles.shape[0], dtype=jnp.int32) < count[0]
    src_take, dest_put, dest_take0, dest_take1, src_put0, src_put1 = [
        jnp.where(live, index, 0).astype(jnp.int32)
        for index in (
            src_half + per * gather_place(*src_at),
            dest_tile + per * scatter_place(*dest_at),
            dest_tile + per * gather_place(*dest_at),
            dest,
            src_half + per * plane,
            src_half + per * scatter_place(*src_at),
        )
    ]

    half = (rows, EDGE)
    full = (rows, width)
    block = [(n_z * rows, EDGE)]
    parts = [features[:, :EDGE], features[:, EDGE:]]
    first = around(parts[0], "z")
    second = around(swap(parts[0], "xl"), "z")
    (both,) = whole_call(
        pair_body,
        [(2 * rows, EDGE)],
        parts[1],
        swap(parts[1], "xl"),
        *second[1:],
        skipped=n_z - 1,
        name="pair1",
    )
    gathered = around(both, "z")
    (first,) = whole_call(join_body, block, *first, name="join0")
    (second,) = whole_call(join_body, block, *second, name="join1")
    partial0 = spread(
        tiles,
        src_take,
        dest_put,
        count,
        [first, second, swap(first, "core"), swap(second, "core")],
        [2 * rows] * n_y,
        False,
        [],
        "forward0",
    )
    (joined,) = whole_call(
        join_pairs_body, [(half_tiles * EDGE, EDGE)], *gathered, partial0[0], skipped=1, name="join2"
    )
    partial1 = spread(
        tiles,
        src_take,
        dest_put,
        count,
        [joined, swap(joined, "core")],
        [rows] * n_row,
        False,
        [],
        "forward1",
    )
    arrived = [offset_send(partial1[offset], ROW_AXES, "y", offset) for offset in range(1, n_row)]
    arrived0 = [ring_send(partial0[step], "y", step) for step in range(1, n_y)]
    own, other = whole_call(
        functools.partial(fold_body, n_y),
        [half, half],
        partial0[0],
        *arrived0,
        arrived[0],
        skipped=1,
        name="fold0",
    )
    piece_rows = 2 * width // n_row
    hidden, grad0, grad1, weight_part = whole_call(
        middle_body,
        [full, half, half, (n_row, piece_rows, EDGE)],
        weight,
        out_grad,
        own,
        swap(other, "xh"),
        partial1[0],
        *arrived,
        name="middle",
    )

    other = swap(grad0, "xh")
    sources0 = around(grad0, "y") + around(other, "y")
    (copied,) = whole_call(
        copies_body, [(n_row, rows + piece_rows, EDGE)], grad1, weight_part, other, skipped=1, name="copies"
    )
    arrived = exchange(copied, ROW_AXES)
    sources1, piece = whole_call(
        unpack_body, [(n_row * rows, EDGE), (piece_rows, EDGE)], arrived, name="unpack"
    )
    mine, other = spread(
        tiles,
        dest_take0,
        src_put0,
        count,
        sources0,
        [half_tiles * EDGE] * 2,
        True,
        [copied],
        "backward0",
    )
    (share,) = whole_call(
        share_body,
        [(n_plane, rows + piece_rows, EDGE)],
        mine,
        swap(other, "core"),
        piece,
        swap(piece, "core"),
        name="share0",
    )
    terms = exchange(share, PLANE_AXES)
    mine, other = spread(
        tiles,
        dest_take1,
        src_put1,
        count,
        [sources1],
        [half_tiles * EDGE] * 2,
        True,
        [share],
        "backward1",
    )
    shares = whole_call(
        functools.partial(add_body, 0, n_plane),
        [half] * n_plane,
        mine,
        swap(other, "core"),
        name="share1",
    )
    arrived = [offset_send(shares[offset], PLANE_AXES, "z", offset) for offset in range(1, n_plane)]
    grad_x0, piece = whole_call(sum_body, [half, (piece_rows, EDGE)], terms, name="sum0")
    (grad_x,) = whole_call(finish_body, [full], grad_x0, shares[0], *arrived, name="finish")

    pieces = exchange(jnp.broadcast_to(piece[None], (n_row, piece_rows, EDGE)), ROW_AXES)
    scale = (rows * n_row * n_col) ** (-0.5)
    (grad_w,) = whole_call(functools.partial(assemble_body, scale), [full], pieces, name="assemble")
    return hidden, grad_x, grad_w


def solution(mesh):
    chips = Mesh(mesh.devices.reshape(4, 2, 2, 4, 2), ROW_AXES + COL_AXES)
    placed = (
        P(ROW_AXES + COL_AXES, None),
        P(),
        P(COL_AXES, ROW_AXES, None, None, None),
        P(COL_AXES, ROW_AXES, None, None),
        P(COL_AXES, ROW_AXES),
        P(COL_AXES + ROW_AXES, None),
    )
    return jax.shard_map(
        body,
        mesh=chips,
        in_specs=placed,
        out_specs=(P(COL_AXES + ROW_AXES, None), P(ROW_AXES + COL_AXES, None), P()),
        check_vma=False,
    )
```

```python
import functools

import jax
import jax.numpy as jnp
from jax import lax
from jax.experimental import pallas as pl
from jax.experimental.pallas import tpu as pltpu
from jax.sharding import Mesh
from jax.sharding import PartitionSpec as P

EDGE = 128
BLOCK = 32
ROW_AXES = ("y", "xh")
COL_AXES = ("xl", "z", "core")
PLANE_AXES = ("xl", "z")
VMEM_LIMIT = 40 << 20


def split(value):
    high = value.astype(jnp.bfloat16)
    low = (value - high.astype(jnp.float32)).astype(jnp.bfloat16)
    return high, low


def dot3(left, right, dims=((1,), (0,))):
    dot = functools.partial(
        lax.dot_general, dimension_numbers=(dims, ((), ())), preferred_element_type=jnp.float32
    )
    left_high, left_low = split(left)
    right_high, right_low = split(right)
    return dot(left_high, right_high) + (dot(left_high, right_low) + dot(left_low, right_high))


def spread_body(flipped, n_src, n_out, take, put, count, tiles, *refs):
    sources, outs = refs[:n_src], refs[-4 - n_out : -4]
    paired, total, held, arrived = refs[-4:]
    slots = held.shape[0]

    def fetch(index):
        here = pl.ds(index * BLOCK, BLOCK)
        return pltpu.make_async_copy(tiles.at[here], held.at[here], arrived.at[index])

    for index in range(slots // BLOCK):

        @pl.when(index * BLOCK < count[0])
        def _(index=index):
            fetch(index).start()

    total[...] = jnp.zeros_like(total)
    first = 0
    for source in sources:
        rows = source.shape[0] // EDGE

        def pair(index, carry, source=source, first=first):
            high, low = split(source[pl.ds(pl.multiple_of(index * EDGE, EDGE), EDGE), :])
            paired[first + index, :EDGE, :EDGE] = high
            paired[first + index, :EDGE, EDGE:] = low
            paired[first + index, EDGE:, :EDGE] = high
            paired[first + index, EDGE:, EDGE:] = jnp.zeros_like(low)
            return carry

        lax.fori_loop(0, rows, pair, 0)
        first += rows

    def block(index, masked):
        for offset in range(BLOCK):
            slot = index * BLOCK + offset
            tile = held[slot]
            if masked:
                tile = jnp.where(slot < count[0], tile, 0.0)
            high, low = split(tile.T if flipped else tile)
            both = jnp.dot(
                jnp.concatenate([high, low], axis=1),
                paired[take[slot]],
                preferred_element_type=jnp.float32,
            )
            total[put[slot]] += both[:, :EDGE] + both[:, EDGE:]

    def whole_block(index, carry):
        fetch(index).wait()
        block(index, False)
        return carry

    blocks = count[0] // BLOCK
    lax.fori_loop(0, blocks, whole_block, 0)

    @pl.when(blocks * BLOCK < count[0])
    def _():
        fetch(blocks).wait()
        block(blocks, True)

    place = 0
    for out in outs:
        for index in range(out.shape[0] // EDGE):
            out[index * EDGE : (index + 1) * EDGE] = total[place + index]
        place += out.shape[0] // EDGE


def spread(tiles, take, put, count, sources, out_rows, flipped, after, name):
    slots = tiles.shape[0]
    src_count = sum(source.shape[0] // EDGE for source in sources)
    scalars, here = pl.BlockSpec(memory_space=pltpu.SMEM), pl.BlockSpec(memory_space=pltpu.VMEM)
    there = pl.BlockSpec(memory_space=pl.ANY)
    return pl.pallas_call(
        functools.partial(spread_body, flipped, len(sources), len(out_rows)),
        in_specs=[scalars] * 3 + [there] + [here] * len(sources) + [there] * len(after),
        out_specs=[here] * len(out_rows),
        scratch_shapes=[
            pltpu.VMEM((src_count, 2 * EDGE, 2 * EDGE), jnp.bfloat16),
            pltpu.VMEM((sum(out_rows) // EDGE, EDGE, EDGE), jnp.float32),
            pltpu.VMEM(tiles.shape, jnp.float32),
            pltpu.SemaphoreType.DMA((slots // BLOCK,)),
        ],
        out_shape=[jax.ShapeDtypeStruct((n, EDGE), jnp.float32) for n in out_rows],
        compiler_params=pltpu.CompilerParams(vmem_limit_bytes=VMEM_LIMIT),
        cost_estimate=pl.CostEstimate(flops=0, bytes_accessed=0, transcendentals=0),
        name=name,
    )(take, put, count, tiles, *sources, *after)


def whole_call(kernel, outs, *args, skipped=0, name):
    here, there = pl.BlockSpec(memory_space=pltpu.VMEM), pl.BlockSpec(memory_space=pl.ANY)
    return pl.pallas_call(
        kernel,
        in_specs=[here] * (len(args) - skipped) + [there] * skipped,
        out_specs=[here] * len(outs),
        out_shape=[jax.ShapeDtypeStruct(shape, jnp.float32) for shape in outs],
        compiler_params=pltpu.CompilerParams(vmem_limit_bytes=VMEM_LIMIT),
        name=name,
    )(*args)


def added(terms):
    return functools.reduce(lambda left, right: left + right, [term[...] for term in terms])


def middle_body(weight, out_grad, own, other, *refs):
    terms, (hidden, grad0, grad1, weight_part) = refs[:-4], refs[-4:]
    mixed = jnp.concatenate([own[...] + other[...], added(terms)], axis=1)
    pre_act = dot3(mixed, weight[...])
    sigma = jax.nn.sigmoid(pre_act)
    hidden[...] = pre_act * sigma
    slope = sigma * (1.0 + pre_act * (1.0 - sigma))
    local = out_grad[...] * slope
    back = dot3(local, weight[...], ((1,), (1,)))
    grad0[...] = back[:, :EDGE]
    grad1[...] = back[:, EDGE:]
    term = dot3(mixed, local, ((0,), (0,)))
    count = weight_part.shape[1] // 2
    for place in range(weight_part.shape[0]):
        for side in range(2):
            weight_part[place, side * count : (side + 1) * count, :] = term[
                place * count : (place + 1) * count, side * EDGE : (side + 1) * EDGE
            ]


def copies_body(value, *refs):
    out = refs[-1]
    rows = value.shape[0]
    for place in range(out.shape[0]):
        out[place, :rows] = value[...]
        if out.shape[1] > rows:
            out[place, rows:] = refs[0][place] + refs[1][place]


def unpack_body(arrived, rows_out, piece):
    rows = rows_out.shape[0] // arrived.shape[0]
    for place in range(arrived.shape[0]):
        rows_out[place * rows : (place + 1) * rows] = arrived[place, :rows]
    piece[...] = jnp.sum(arrived[:, rows:], axis=0)


def join_body(*refs):
    blocks, out = refs[:-1], refs[-1]
    rows = blocks[0].shape[0]
    for place, block in enumerate(blocks):
        out[place * rows : (place + 1) * rows] = block[...]


def join_pairs_body(*refs):
    blocks, out = refs[:-2], refs[-1]
    rows = blocks[0].shape[0] // 2
    for place, block in enumerate(blocks):
        for half in range(2):
            first = (half * len(blocks) + place) * rows
            out[first : first + rows] = block[half * rows : (half + 1) * rows]


def pair_body(mine, other, *refs):
    out = refs[-1]
    rows = mine.shape[0]
    out[:rows] = mine[...]
    out[rows:] = other[...]


def fold_body(n_terms, *refs):
    terms, outs = refs[:n_terms], refs[n_terms + 1 :]
    total = added(terms)
    first = 0
    for out in outs:
        out[...] = total[first : first + out.shape[0]]
        first += out.shape[0]


def add_body(count, mine, *refs):
    others, outs = refs[:count], refs[count:]
    for step, (other, out) in enumerate(zip(others, outs)):
        out[...] = mine[pl.ds(step * out.shape[0], out.shape[0]), :] + other[...]


def share_body(mine, other, piece, out):
    rows = out.shape[1] - piece.shape[0]
    for place in range(out.shape[0]):
        here = pl.ds(place * rows, rows)
        out[place, :rows] = mine[here, :] + other[here, :]
        out[place, rows:] = piece[...]


def sum_body(terms, grad, piece):
    total = jnp.sum(terms[...], axis=0)
    rows = grad.shape[0]
    grad[...] = total[:rows]
    piece[...] = total[rows:]


def finish_body(grad0, *refs):
    terms, out = refs[:-1], refs[-1]
    out[:, :EDGE] = grad0[...]
    out[:, EDGE:] = added(terms)


def assemble_body(scale, pieces, out):
    count = pieces.shape[1] // 2
    for place in range(pieces.shape[0]):
        for side in range(2):
            out[place * count : (place + 1) * count, side * EDGE : (side + 1) * EDGE] = (
                pieces[place, side * count : (side + 1) * count, :] * scale
            )


def swap(value, axis):
    return lax.ppermute(value, axis, [(0, 1), (1, 0)])


def ring_send(value, axis, step):
    size = lax.axis_size(axis)
    return lax.ppermute(value, axis, [(place, (place + step) % size) for place in range(size)])


def offset_send(value, axes, ring, offset):
    sizes = [lax.axis_size(axis) for axis in axes]
    hops = []
    for a in range(sizes[0]):
        for b in range(sizes[1]):
            if axes[0] == ring:
                to = (a + offset // 2) % sizes[0], b ^ (offset % 2)
            else:
                to = a ^ (offset % 2), (b + offset // 2) % sizes[1]
            hops.append((a * sizes[1] + b, to[0] * sizes[1] + to[1]))
    return lax.ppermute(value, axes, hops)


def exchange(value, axes):
    return lax.all_to_all(value, axes, 0, 0, tiled=True)


def gather_place(ring_index, pair_index, ring, pair):
    size = lax.axis_size(ring)
    return (pair_index ^ lax.axis_index(pair)) * size + (lax.axis_index(ring) - ring_index) % size


def scatter_place(ring_index, pair_index, ring, pair):
    step = (ring_index - lax.axis_index(ring)) % lax.axis_size(ring)
    return step * 2 + (pair_index ^ lax.axis_index(pair))


def around(value, axis):
    return [value] + [ring_send(value, axis, step) for step in range(1, lax.axis_size(axis))]


def body(features, weight, tile_vals, tile_index, tile_count, out_grad):
    tiles = tile_vals[0, 0]
    dest = tile_index[0, 0, 0]
    src = tile_index[0, 0, 1]
    count = tile_count[0]
    n_row = lax.axis_size(ROW_AXES)
    n_col = lax.axis_size(COL_AXES)
    n_plane = lax.axis_size(PLANE_AXES)
    n_z = lax.axis_size("z")
    n_y = lax.axis_size("y")
    rows, width = features.shape
    per = rows // EDGE
    half_tiles = n_plane * per
    src_home, src_tile = src // per, src % per
    src_half = ((src_home % 2) ^ lax.axis_index("core")) * half_tiles + src_tile
    dest_home, dest_tile = dest // per, dest % per

    plane = src_home // 2

    src_at = (plane % n_z, plane // n_z, "z", "xl")
    dest_at = (dest_home // 2, dest_home % 2, "y", "xh")

    live = jnp.arange(tiles.shape[0], dtype=jnp.int32) < count[0]
    src_take, dest_put, dest_take0, dest_take1, src_put0, src_put1 = [
        jnp.where(live, index, 0).astype(jnp.int32)
        for index in (
            src_half + per * gather_place(*src_at),
            dest_tile + per * scatter_place(*dest_at),
            dest_tile + per * gather_place(*dest_at),
            dest,
            src_half + per * plane,
            src_half + per * scatter_place(*src_at),
        )
    ]

    half = (rows, EDGE)
    full = (rows, width)
    block = [(n_z * rows, EDGE)]
    parts = [features[:, :EDGE], features[:, EDGE:]]
    first = around(parts[0], "z")
    second = around(swap(parts[0], "xl"), "z")
    (both,) = whole_call(
        pair_body,
        [(2 * rows, EDGE)],
        parts[1],
        swap(parts[1], "xl"),
        *second[1:],
        skipped=n_z - 1,
        name="pair1",
    )
    gathered = around(both, "z")
    (first,) = whole_call(join_body, block, *first, name="join0")
    (second,) = whole_call(join_body, block, *second, name="join1")
    partial0 = spread(
        tiles,
        src_take,
        dest_put,
        count,
        [first, second, swap(first, "core"), swap(second, "core")],
        [2 * rows] * n_y,
        False,
        [],
        "forward0",
    )
    (joined,) = whole_call(
        join_pairs_body, [(half_tiles * EDGE, EDGE)], *gathered, partial0[0], skipped=1, name="join2"
    )
    partial1 = spread(
        tiles,
        src_take,
        dest_put,
        count,
        [joined, swap(joined, "core")],
        [rows] * n_row,
        False,
        [],
        "forward1",
    )
    arrived = [offset_send(partial1[offset], ROW_AXES, "y", offset) for offset in range(1, n_row)]
    arrived0 = [ring_send(partial0[step], "y", step) for step in range(1, n_y)]
    own, other = whole_call(
        functools.partial(fold_body, n_y),
        [half, half],
        partial0[0],
        *arrived0,
        arrived[0],
        skipped=1,
        name="fold0",
    )
    piece_rows = 2 * width // n_row
    hidden, grad0, grad1, weight_part = whole_call(
        middle_body,
        [full, half, half, (n_row, piece_rows, EDGE)],
        weight,
        out_grad,
        own,
        swap(other, "xh"),
        partial1[0],
        *arrived,
        name="middle",
    )

    other = swap(grad0, "xh")
    sources0 = around(grad0, "y") + around(other, "y")
    (copied,) = whole_call(
        copies_body,
        [(n_row, rows + piece_rows, EDGE)],
        grad1,
        weight_part,
        swap(weight_part, "core"),
        other,
        skipped=1,
        name="copies",
    )
    arrived = exchange(copied, ROW_AXES)
    sources1, piece = whole_call(
        unpack_body, [(n_row * rows, EDGE), (piece_rows, EDGE)], arrived, name="unpack"
    )
    mine, other = spread(
        tiles,
        dest_take0,
        src_put0,
        count,
        sources0,
        [half_tiles * EDGE] * 2,
        True,
        [copied],
        "backward0",
    )
    (share,) = whole_call(
        share_body,
        [(n_plane, rows + piece_rows, EDGE)],
        mine,
        swap(other, "core"),
        piece,
        name="share0",
    )
    terms = exchange(share, PLANE_AXES)
    mine, *others = spread(
        tiles,
        dest_take1,
        src_put1,
        count,
        [sources1],
        [half_tiles * EDGE] + [2 * rows] * n_z,
        True,
        [share],
        "backward1",
    )
    shares = whole_call(
        functools.partial(add_body, n_z),
        [(2 * rows, EDGE)] * n_z,
        mine,
        *[swap(other, "core") for other in others],
        name="share1",
    )
    arrived = [ring_send(shares[step], "z", step) for step in range(1, n_z)]
    own, other = whole_call(
        functools.partial(fold_body, n_z), [half, half], shares[0], *arrived, mine, skipped=1, name="fold1"
    )
    grad_x0, piece = whole_call(sum_body, [half, (piece_rows, EDGE)], terms, name="sum0")
    (grad_x,) = whole_call(finish_body, [full], grad_x0, own, swap(other, "xl"), name="finish")

    pieces = exchange(jnp.broadcast_to(piece[None], (n_row, piece_rows, EDGE)), ROW_AXES)
    scale = (rows * n_row * n_col) ** (-0.5)
    (grad_w,) = whole_call(functools.partial(assemble_body, scale), [full], pieces, name="assemble")
    return hidden, grad_x, grad_w


def solution(mesh):
    chips = Mesh(mesh.devices.reshape(4, 2, 2, 4, 2), ROW_AXES + COL_AXES)
    placed = (
        P(ROW_AXES + COL_AXES, None),
        P(),
        P(COL_AXES, ROW_AXES, None, None, None),
        P(COL_AXES, ROW_AXES, None, None),
        P(COL_AXES, ROW_AXES),
        P(COL_AXES + ROW_AXES, None),
    )
    return jax.shard_map(
        body,
        mesh=chips,
        in_specs=placed,
        out_specs=(P(COL_AXES + ROW_AXES, None), P(ROW_AXES + COL_AXES, None), P()),
        check_vma=False,
    )
```

```python
import functools

import jax
import jax.numpy as jnp
from jax import lax
from jax.experimental import pallas as pl
from jax.experimental.pallas import tpu as pltpu
from jax.sharding import Mesh
from jax.sharding import PartitionSpec as P

EDGE = 128
BLOCK = 32
ROW_AXES = ("y", "xh")
COL_AXES = ("xl", "z", "core")
PLANE_AXES = ("xl", "z")
VMEM_LIMIT = 40 << 20


def split(value):
    high = value.astype(jnp.bfloat16)
    low = (value - high.astype(jnp.float32)).astype(jnp.bfloat16)
    return high, low


def dot3(left, right, dims=((1,), (0,))):
    dot = functools.partial(
        lax.dot_general, dimension_numbers=(dims, ((), ())), preferred_element_type=jnp.float32
    )
    left_high, left_low = split(left)
    right_high, right_low = split(right)
    return dot(left_high, right_high) + (dot(left_high, right_low) + dot(left_low, right_high))


def spread_body(flipped, n_src, n_out, take, put, count, tiles, *refs):
    sources, outs = refs[:n_src], refs[-4 - n_out : -4]
    paired, total, held, arrived = refs[-4:]
    slots = held.shape[0]

    def fetch(index):
        here = pl.ds(index * BLOCK, BLOCK)
        return pltpu.make_async_copy(tiles.at[here], held.at[here], arrived.at[index])

    for index in range(slots // BLOCK):

        @pl.when(index * BLOCK < count[0])
        def _(index=index):
            fetch(index).start()

    total[...] = jnp.zeros_like(total)
    first = 0
    for source in sources:
        rows = source.shape[0] // EDGE

        def pair(index, carry, source=source, first=first):
            high, low = split(source[pl.ds(pl.multiple_of(index * EDGE, EDGE), EDGE), :])
            paired[first + index, :EDGE, :EDGE] = high
            paired[first + index, :EDGE, EDGE:] = low
            paired[first + index, EDGE:, :EDGE] = high
            paired[first + index, EDGE:, EDGE:] = jnp.zeros_like(low)
            return carry

        lax.fori_loop(0, rows, pair, 0)
        first += rows

    def block(index, carry):
        fetch(index).wait()
        for offset in range(BLOCK):
            slot = index * BLOCK + offset
            high, low = split(held[slot].T if flipped else held[slot])
            high = jnp.where(slot < count[0], high, jnp.zeros_like(high))
            low = jnp.where(slot < count[0], low, jnp.zeros_like(low))
            both = jnp.dot(
                jnp.concatenate([high, low], axis=1),
                paired[take[slot]],
                preferred_element_type=jnp.float32,
            )
            total[put[slot]] += both[:, :EDGE] + both[:, EDGE:]
        return carry

    lax.fori_loop(0, pl.cdiv(count[0], BLOCK), block, 0)

    place = 0
    for out in outs:
        for index in range(out.shape[0] // EDGE):
            out[index * EDGE : (index + 1) * EDGE] = total[place + index]
        place += out.shape[0] // EDGE


def spread(tiles, take, put, count, sources, out_rows, flipped, after, name):
    slots = tiles.shape[0]
    src_count = sum(source.shape[0] // EDGE for source in sources)
    scalars, here = pl.BlockSpec(memory_space=pltpu.SMEM), pl.BlockSpec(memory_space=pltpu.VMEM)
    there = pl.BlockSpec(memory_space=pl.ANY)
    return pl.pallas_call(
        functools.partial(spread_body, flipped, len(sources), len(out_rows)),
        in_specs=[scalars] * 3 + [there] + [here] * len(sources) + [there] * len(after),
        out_specs=[here] * len(out_rows),
        scratch_shapes=[
            pltpu.VMEM((src_count, 2 * EDGE, 2 * EDGE), jnp.bfloat16),
            pltpu.VMEM((sum(out_rows) // EDGE, EDGE, EDGE), jnp.float32),
            pltpu.VMEM(tiles.shape, jnp.float32),
            pltpu.SemaphoreType.DMA((slots // BLOCK,)),
        ],
        out_shape=[jax.ShapeDtypeStruct((n, EDGE), jnp.float32) for n in out_rows],
        compiler_params=pltpu.CompilerParams(vmem_limit_bytes=VMEM_LIMIT),
        cost_estimate=pl.CostEstimate(flops=0, bytes_accessed=0, transcendentals=0),
        name=name,
    )(take, put, count, tiles, *sources, *after)


def whole_call(kernel, outs, *args, skipped=0, name):
    here, there = pl.BlockSpec(memory_space=pltpu.VMEM), pl.BlockSpec(memory_space=pl.ANY)
    return pl.pallas_call(
        kernel,
        in_specs=[here] * (len(args) - skipped) + [there] * skipped,
        out_specs=[here] * len(outs),
        out_shape=[jax.ShapeDtypeStruct(shape, jnp.float32) for shape in outs],
        compiler_params=pltpu.CompilerParams(vmem_limit_bytes=VMEM_LIMIT),
        name=name,
    )(*args)


def added(terms):
    return functools.reduce(lambda left, right: left + right, [term[...] for term in terms])


def middle_body(weight, out_grad, own, other, *refs):
    terms, (hidden, grad0, grad1, weight_part) = refs[:-4], refs[-4:]
    mixed = jnp.concatenate([own[...] + other[...], added(terms)], axis=1)
    pre_act = dot3(mixed, weight[...])
    sigma = jax.nn.sigmoid(pre_act)
    hidden[...] = pre_act * sigma
    slope = sigma * (1.0 + pre_act * (1.0 - sigma))
    local = out_grad[...] * slope
    back = dot3(local, weight[...], ((1,), (1,)))
    grad0[...] = back[:, :EDGE]
    grad1[...] = back[:, EDGE:]
    term = dot3(mixed, local, ((0,), (0,)))
    count = weight_part.shape[1] // 2
    for place in range(weight_part.shape[0]):
        for side in range(2):
            weight_part[place, side * count : (side + 1) * count, :] = term[
                place * count : (place + 1) * count, side * EDGE : (side + 1) * EDGE
            ]


def copies_body(value, *refs):
    out = refs[-1]
    rows = value.shape[0]
    for place in range(out.shape[0]):
        out[place, :rows] = value[...]
        if out.shape[1] > rows:
            out[place, rows:] = refs[0][place] + refs[1][place]


def unpack_body(arrived, rows_out, piece):
    rows = rows_out.shape[0] // arrived.shape[0]
    for place in range(arrived.shape[0]):
        rows_out[place * rows : (place + 1) * rows] = arrived[place, :rows]
    piece[...] = jnp.sum(arrived[:, rows:], axis=0)


def join_body(*refs):
    blocks, out = refs[:-1], refs[-1]
    rows = blocks[0].shape[0]
    for place, block in enumerate(blocks):
        out[place * rows : (place + 1) * rows] = block[...]


def join_pairs_body(*refs):
    blocks, out = refs[:-2], refs[-1]
    rows = blocks[0].shape[0] // 2
    for place, block in enumerate(blocks):
        for half in range(2):
            first = (half * len(blocks) + place) * rows
            out[first : first + rows] = block[half * rows : (half + 1) * rows]


def pair_body(mine, other, *refs):
    out = refs[-1]
    rows = mine.shape[0]
    out[:rows] = mine[...]
    out[rows:] = other[...]


def fold_body(n_terms, *refs):
    terms, outs = refs[:n_terms], refs[n_terms + 1 :]
    total = added(terms)
    first = 0
    for out in outs:
        out[...] = total[first : first + out.shape[0]]
        first += out.shape[0]


def add_body(count, mine, *refs):
    others, outs = refs[:count], refs[count:]
    for step, (other, out) in enumerate(zip(others, outs)):
        out[...] = mine[pl.ds(step * out.shape[0], out.shape[0]), :] + other[...]


def share_body(mine, other, piece, out):
    rows = out.shape[1] - piece.shape[0]
    for place in range(out.shape[0]):
        here = pl.ds(place * rows, rows)
        out[place, :rows] = mine[here, :] + other[here, :]
        out[place, rows:] = piece[...]


def sum_body(terms, grad, piece):
    total = jnp.sum(terms[...], axis=0)
    rows = grad.shape[0]
    grad[...] = total[:rows]
    piece[...] = total[rows:]


def finish_body(grad0, *refs):
    terms, out = refs[:-1], refs[-1]
    out[:, :EDGE] = grad0[...]
    out[:, EDGE:] = added(terms)


def assemble_body(scale, pieces, out):
    count = pieces.shape[1] // 2
    for place in range(pieces.shape[0]):
        for side in range(2):
            out[place * count : (place + 1) * count, side * EDGE : (side + 1) * EDGE] = (
                pieces[place, side * count : (side + 1) * count, :] * scale
            )


def swap(value, axis):
    return lax.ppermute(value, axis, [(0, 1), (1, 0)])


def ring_send(value, axis, step):
    size = lax.axis_size(axis)
    return lax.ppermute(value, axis, [(place, (place + step) % size) for place in range(size)])


def offset_send(value, axes, ring, offset):
    sizes = [lax.axis_size(axis) for axis in axes]
    hops = []
    for a in range(sizes[0]):
        for b in range(sizes[1]):
            if axes[0] == ring:
                to = (a + offset // 2) % sizes[0], b ^ (offset % 2)
            else:
                to = a ^ (offset % 2), (b + offset // 2) % sizes[1]
            hops.append((a * sizes[1] + b, to[0] * sizes[1] + to[1]))
    return lax.ppermute(value, axes, hops)


def exchange(value, axes):
    return lax.all_to_all(value, axes, 0, 0, tiled=True)


def gather_place(ring_index, pair_index, ring, pair):
    size = lax.axis_size(ring)
    return (pair_index ^ lax.axis_index(pair)) * size + (lax.axis_index(ring) - ring_index) % size


def scatter_place(ring_index, pair_index, ring, pair):
    step = (ring_index - lax.axis_index(ring)) % lax.axis_size(ring)
    return step * 2 + (pair_index ^ lax.axis_index(pair))


def around(value, axis):
    return [value] + [ring_send(value, axis, step) for step in range(1, lax.axis_size(axis))]


def body(features, weight, tile_vals, tile_index, tile_count, out_grad):
    tiles = tile_vals[0, 0]
    dest = tile_index[0, 0, 0]
    src = tile_index[0, 0, 1]
    count = tile_count[0]
    n_row = lax.axis_size(ROW_AXES)
    n_col = lax.axis_size(COL_AXES)
    n_plane = lax.axis_size(PLANE_AXES)
    n_z = lax.axis_size("z")
    n_y = lax.axis_size("y")
    rows, width = features.shape
    per = rows // EDGE
    half_tiles = n_plane * per
    src_home, src_tile = src // per, src % per
    src_half = ((src_home % 2) ^ lax.axis_index("core")) * half_tiles + src_tile
    dest_home, dest_tile = dest // per, dest % per

    plane = src_home // 2

    src_at = (plane % n_z, plane // n_z, "z", "xl")
    dest_at = (dest_home // 2, dest_home % 2, "y", "xh")

    live = jnp.arange(tiles.shape[0], dtype=jnp.int32) < count[0]
    src_take, dest_put, dest_take0, dest_take1, src_put0, src_put1 = [
        jnp.where(live, index, 0).astype(jnp.int32)
        for index in (
            src_half + per * gather_place(*src_at),
            dest_tile + per * scatter_place(*dest_at),
            dest_tile + per * gather_place(*dest_at),
            dest,
            src_half + per * plane,
            src_half + per * scatter_place(*src_at),
        )
    ]

    half = (rows, EDGE)
    full = (rows, width)
    block = [(n_z * rows, EDGE)]
    parts = [features[:, :EDGE], features[:, EDGE:]]
    first = around(parts[0], "z")
    second = around(swap(parts[0], "xl"), "z")
    (both,) = whole_call(
        pair_body,
        [(2 * rows, EDGE)],
        parts[1],
        swap(parts[1], "xl"),
        *second[1:],
        skipped=n_z - 1,
        name="pair1",
    )
    gathered = around(both, "z")
    (first,) = whole_call(join_body, block, *first, name="join0")
    (second,) = whole_call(join_body, block, *second, name="join1")
    partial0 = spread(
        tiles,
        src_take,
        dest_put,
        count,
        [first, second, swap(first, "core"), swap(second, "core")],
        [2 * rows] * n_y,
        False,
        [],
        "forward0",
    )
    (joined,) = whole_call(
        join_pairs_body, [(half_tiles * EDGE, EDGE)], *gathered, partial0[0], skipped=1, name="join2"
    )
    partial1 = spread(
        tiles,
        src_take,
        dest_put,
        count,
        [joined, swap(joined, "core")],
        [rows] * n_row,
        False,
        [],
        "forward1",
    )
    arrived = [offset_send(partial1[offset], ROW_AXES, "y", offset) for offset in range(1, n_row)]
    arrived0 = [ring_send(partial0[step], "y", step) for step in range(1, n_y)]
    own, other = whole_call(
        functools.partial(fold_body, n_y),
        [half, half],
        partial0[0],
        *arrived0,
        arrived[0],
        skipped=1,
        name="fold0",
    )
    piece_rows = 2 * width // n_row
    hidden, grad0, grad1, weight_part = whole_call(
        middle_body,
        [full, half, half, (n_row, piece_rows, EDGE)],
        weight,
        out_grad,
        own,
        swap(other, "xh"),
        partial1[0],
        *arrived,
        name="middle",
    )

    other = swap(grad0, "xh")
    sources0 = around(grad0, "y") + around(other, "y")
    (copied,) = whole_call(
        copies_body,
        [(n_row, rows + piece_rows, EDGE)],
        grad1,
        weight_part,
        swap(weight_part, "core"),
        name="copies",
    )
    arrived = exchange(copied, ROW_AXES)
    sources1, piece = whole_call(
        unpack_body, [(n_row * rows, EDGE), (piece_rows, EDGE)], arrived, name="unpack"
    )
    mine, other = spread(
        tiles,
        dest_take0,
        src_put0,
        count,
        sources0,
        [half_tiles * EDGE] * 2,
        True,
        [copied],
        "backward0",
    )
    (share,) = whole_call(
        share_body,
        [(n_plane, rows + piece_rows, EDGE)],
        mine,
        swap(other, "core"),
        piece,
        name="share0",
    )
    terms = exchange(share, PLANE_AXES)
    mine, *others = spread(
        tiles,
        dest_take1,
        src_put1,
        count,
        [sources1],
        [half_tiles * EDGE] + [2 * rows] * n_z,
        True,
        [share],
        "backward1",
    )
    shares = whole_call(
        functools.partial(add_body, n_z),
        [(2 * rows, EDGE)] * n_z,
        mine,
        *[swap(other, "core") for other in others],
        name="share1",
    )
    arrived = [ring_send(shares[step], "z", step) for step in range(1, n_z)]
    own, other = whole_call(
        functools.partial(fold_body, n_z), [half, half], shares[0], *arrived, mine, skipped=1, name="fold1"
    )
    grad_x0, piece = whole_call(sum_body, [half, (piece_rows, EDGE)], terms, name="sum0")
    (grad_x,) = whole_call(finish_body, [full], grad_x0, own, swap(other, "xl"), name="finish")

    pieces = exchange(jnp.broadcast_to(piece[None], (n_row, piece_rows, EDGE)), ROW_AXES)
    scale = (rows * n_row * n_col) ** (-0.5)
    (grad_w,) = whole_call(functools.partial(assemble_body, scale), [full], pieces, name="assemble")
    return hidden, grad_x, grad_w


def solution(mesh):
    chips = Mesh(mesh.devices.reshape(4, 2, 2, 4, 2), ROW_AXES + COL_AXES)
    placed = (
        P(ROW_AXES + COL_AXES, None),
        P(),
        P(COL_AXES, ROW_AXES, None, None, None),
        P(COL_AXES, ROW_AXES, None, None),
        P(COL_AXES, ROW_AXES),
        P(COL_AXES + ROW_AXES, None),
    )
    return jax.shard_map(
        body,
        mesh=chips,
        in_specs=placed,
        out_specs=(P(COL_AXES + ROW_AXES, None), P(ROW_AXES + COL_AXES, None), P()),
        check_vma=False,
    )
```
